768 devices in a mesh: wide: 16 (over x_lo, y), narrow: 48 (over x_hi, z, core).
Axes of the slice: x: 4 (x_hi: 2, x_lo: 2; x = x_hi * 2 + x_lo), y: 8, z: 12, core: 2. Of those that a mesh axis runs over, the one named last changes fastest.
Arguments:
- features: bfloat16 [48, 2048, 128], P('narrow', 'wide'), may hold values from -6 to 6
- in_weight: bfloat16 [128, 256], replicated, may hold values from -0.5 to 0.5
- hidden_bias: float32 [256], replicated, may hold values from -4 to 4
- classifier: bfloat16 [256, 172], replicated
- adjacency_tiles: bfloat16 [768, 48, 2, 128, 128], P('wide', 'narrow'), may hold values from -0.375 to 0.375
- tile_col: int32 [768, 48, 2], P('wide', 'narrow'), may hold values from 0 to 15, as said below
- tile_count: int32 [768, 48], P('wide', 'narrow'), may hold values from 1 to 2, as said below
- node_perm: int32 [48, 2048], P('narrow', 'wide'), may hold values from 0 to 2047, as said below
- labels: int32 [98304], P(('wide', 'narrow')), may hold values from 0 to 171
Outputs:
- next_input: bfloat16 [48, 2048, 256], P('narrow', 'wide')
- node_loss: float32 [98304], P(('wide', 'narrow'))
- input_grad: float32 [48, 2048, 128], P('narrow', 'wide')
The draws below stay inside these ranges and needn't reach their ends.
Inputs may be any that keep to these rules, and one draw needn't show every extreme that they name: `tile_col`: within one block row and one column group the 2 entries are distinct. `tile_count`: on every device one of its block rows has all 2 slots live. `node_perm`: each row is a permutation of 0 to 2047; of the 128 entries from j * 128 to (j + 1) * 128 - 1, at most 12 lie in any one range d * 128 to (d + 1) * 128 - 1, and exactly 12 in some range.
All inputs are finite; a program needn't handle non-finite values.
Results may differ from the reference program's by a relative error of at most 0.023.
Values may be sent and summed in bfloat16 or wider, within the bound.
A program may use at most 64 MiB of HBM per device.

```python
import math
import jax
import jax.numpy as jnp
from jax import lax

NODE_DEV = 128
TILE = 128
F_IN = 128
HID = 256
CLASSES = 172
GROUP = 2048
NODES = 98304
BLOCKS = 768
ROWBLK = 48
COLBLK = 16
TILES = 2
N_WIDE = 16
N_NARROW = 48


def draw_classifier(key, part):
    key = jax.random.fold_in(key, 11)
    first = jax.random.fold_in(key, 0)
    base = jax.random.normal(first, (HID, CLASSES), jnp.float32) * (4.0 / math.sqrt(HID))
    return base.astype(jnp.bfloat16)


def column_order(key):
    return jax.random.permutation(key, COLBLK)


def draw_tile_col(key, part):
    key = jax.random.fold_in(key, 5)
    keys = jax.random.split(key, BLOCKS * N_NARROW)
    orders = jax.vmap(column_order)(keys)
    return orders[:, :TILES].reshape(BLOCKS, N_NARROW, TILES).astype(jnp.int32)


def draw_tile_count(key, part):
    key = jax.random.fold_in(key, 7)
    first, second, third = jax.random.split(key, 3)
    level = jax.random.randint(first, (N_WIDE, 1, N_NARROW), 1, TILES + 1)
    lowest = (level + 1) // 2
    counts = jax.random.randint(second, (N_WIDE, ROWBLK, N_NARROW), lowest, level + 1)
    full_row = jax.random.randint(third, (N_WIDE, 1, N_NARROW), 0, ROWBLK)
    row_ids = jnp.arange(ROWBLK).reshape(1, ROWBLK, 1)
    counts = jnp.where(row_ids == full_row, TILES, counts)
    return counts.reshape(N_WIDE * ROWBLK, N_NARROW).astype(jnp.int32)


def node_order(key):
    return jax.random.permutation(key, NODE_DEV)


def relay_group(key):
    share = NODE_DEV // N_WIDE
    peer_ids = jnp.arange(N_WIDE)
    pattern = jnp.array([share + share // 2, share - share // 2, share + share // 4, share - share // 4], jnp.int32)
    weights = pattern[peer_ids % 4]
    first, second, third, fourth = jax.random.split(key, 4)
    row_shift = jax.random.permutation(first, N_WIDE)
    col_names = jax.random.permutation(second, N_WIDE)
    latin = col_names[(row_shift[:, None] + peer_ids[None, :]) % N_WIDE]
    bounds = jnp.cumsum(weights)
    places = jnp.arange(NODE_DEV)
    kind_of = jnp.sum((places[:, None] >= bounds[None, :]).astype(jnp.int32), axis=1)
    dest_sorted = latin[:, kind_of]
    shuffles = jax.vmap(node_order)(jax.random.split(third, N_WIDE))
    dest = jnp.take_along_axis(dest_sorted, shuffles, axis=1)
    onehot = (dest[:, :, None] == peer_ids[None, None, :]).astype(jnp.int32)
    slot_rank = jnp.sum((jnp.cumsum(onehot, axis=1) - onehot) * onehot, axis=2)
    counts = jnp.sum(onehot, axis=1)
    before = jnp.cumsum(counts, axis=0) - counts
    offset = jnp.sum(before[:, None, :] * onehot, axis=2)
    within = offset + slot_rank
    arrange = jax.vmap(node_order)(jax.random.split(fourth, N_WIDE))
    slot_value = arrange[dest, within]
    return (dest * NODE_DEV + slot_value).reshape(GROUP).astype(jnp.int32)


def draw_node_perm(key, part):
    key = jax.random.fold_in(key, 9)
    keys = jax.random.split(key, N_NARROW)
    return jax.vmap(relay_group)(keys).astype(jnp.int32)


def touch_ends(entries, key, low, top_value):
    dims = entries.shape
    index_at = [jax.random.randint(jax.random.fold_in(key, axis), (), 0, dims[axis]) for axis in range(len(dims))]
    entries = entries.at[tuple(index_at)].set(low)
    longest = dims.index(max(dims))
    index_at[longest] = (index_at[longest] + 1) % dims[longest]
    return entries.at[tuple(index_at)].set(top_value)


def shard_levels(rng, extent, cuts, low, high):
    level = 1.0
    for dim, shards_of in cuts:
        steps = jax.random.uniform(jax.random.fold_in(jax.random.fold_in(rng, 6), dim), (shards_of,), jnp.float32, low / len(cuts), high / len(cuts))
        level = level * jnp.repeat(jnp.exp(steps), extent[dim] // shards_of).reshape((-1,) + (1,) * (len(extent) - 1 - dim))
    return level


def noise(own_key, extent, width, limit, cuts=(), kind=jnp.bfloat16):
    level = shard_levels(own_key, extent, cuts, -0.22, 0.18) if cuts else 1.0
    entries = jax.random.normal(own_key, extent, jnp.float32) * width * level
    return jnp.minimum(jnp.maximum(entries, -limit), limit).astype(kind)


def setup_inputs(seed: int = 0) -> dict:
    key_of = jax.random.split(jax.random.key(seed), 10)
    features = noise(key_of[0], (N_NARROW, GROUP, F_IN), 1.0, 6.0, ((0, 48), (1, 16)))
    in_weight = noise(key_of[1], (F_IN, HID), F_IN ** -0.5, 0.5)
    hidden_bias = noise(key_of[2], (HID,), 1.0, 4.0, (), jnp.float32)
    classifier = draw_classifier(jax.random.fold_in(key_of[9], 71), 0)
    adjacency_tiles = noise(key_of[4], (BLOCKS, N_NARROW, TILES, TILE, TILE), (TILE * TILES) ** -0.5, 0.375, ((0, 16), (1, 48)))
    tile_col = draw_tile_col(jax.random.fold_in(key_of[9], 71), 0)
    tile_count = draw_tile_count(jax.random.fold_in(key_of[9], 71), 0)
    node_perm = draw_node_perm(jax.random.fold_in(key_of[9], 71), 0)
    labels = touch_ends(jax.random.randint(key_of[8], (NODES,), 0, CLASSES), jax.random.fold_in(key_of[8], 1), 0, CLASSES - 1).astype(jnp.int32)
    return dict(features=features, in_weight=in_weight, hidden_bias=hidden_bias, classifier=classifier, adjacency_tiles=adjacency_tiles, tile_col=tile_col, tile_count=tile_count, node_perm=node_perm, labels=labels)


finest = lax.Precision.HIGHEST


def score_nodes(hidden_pre, classifier, labels):
    gate_value = jax.nn.sigmoid(hidden_pre)
    activated = (hidden_pre * gate_value).astype(jnp.bfloat16)
    logits = jnp.dot(activated, classifier, preferred_element_type=jnp.float32)
    top_score = jnp.max(logits, axis=1, keepdims=True)
    shifted = jnp.exp(logits - top_score)
    exp_total = jnp.sum(shifted, axis=1, keepdims=True)
    target = labels[:, None] == jnp.arange(logits.shape[1])[None, :]
    picked = jnp.sum(jnp.where(target, logits, jnp.zeros_like(logits)), axis=1)
    node_loss = top_score[:, 0] + jnp.log(exp_total[:, 0]) - picked
    grad_logits = shifted / exp_total - target.astype(jnp.float32)
    grad_act = jnp.dot(grad_logits, classifier.astype(jnp.float32).T, precision=finest)
    grad_pre = (grad_act * gate_value * (1.0 + hidden_pre * (1.0 - gate_value))).astype(jnp.bfloat16)
    return activated, node_loss, grad_pre


def reference(features, in_weight, hidden_bias, classifier, adjacency_tiles, tile_col, tile_count, node_perm, labels):
    weight_wide = in_weight.astype(jnp.float32)
    group_inputs = features.astype(jnp.float32).reshape(N_NARROW, COLBLK, TILE, F_IN)
    group_ids = jnp.arange(N_NARROW).astype(jnp.int32)[:, None]
    slot_ids = jnp.arange(TILES).astype(jnp.int32)[None, :]

    def block_row(pieces):
        blocks, columns, counts = pieces
        live_slots = (slot_ids < counts[:, None]).astype(jnp.float32)
        chosen = group_inputs[group_ids, columns.astype(jnp.int32)]
        masked = blocks.astype(jnp.float32) * live_slots[:, :, None, None]
        return jnp.einsum("ctik,ctkf->if", masked, chosen, precision=finest)

    aggregated = lax.map(block_row, (adjacency_tiles, tile_col, tile_count)).reshape(NODES, F_IN)
    hidden_pre = jnp.dot(aggregated, weight_wide, precision=finest) + hidden_bias
    activated, node_loss, grad_pre = score_nodes(hidden_pre, classifier, labels)
    backward_rows = jnp.dot(grad_pre.astype(jnp.float32), weight_wide.T, precision=finest)
    backward_rows = backward_rows.reshape(BLOCKS, TILE, F_IN)

    def add_block_row(carried, pieces):
        blocks, columns, counts, rows = pieces
        live_slots = (slot_ids < counts[:, None]).astype(jnp.float32)
        masked = blocks.astype(jnp.float32) * live_slots[:, :, None, None]
        part = jnp.einsum("ctik,if->ctkf", masked, rows, precision=finest)
        return carried.at[group_ids, columns.astype(jnp.int32)].add(part), None

    start_grad = jnp.zeros((N_NARROW, COLBLK, TILE, F_IN), jnp.float32)
    summed_grad, unused = lax.scan(add_block_row, start_grad, (adjacency_tiles, tile_col, tile_count, backward_rows))
    input_grad = summed_grad.reshape(N_NARROW, GROUP, F_IN)
    by_group = activated.reshape(N_WIDE, N_NARROW, NODE_DEV, HID).transpose(1, 0, 2, 3).reshape(N_NARROW, GROUP, HID)
    inverse = jnp.argsort(node_perm, axis=1).astype(jnp.int32)
    next_input = jnp.take_along_axis(by_group, inverse[:, :, None], axis=1)
    return next_input, node_loss, input_grad
```

```python
import functools

import jax
import jax.numpy as jnp
from jax import lax
from jax.experimental import pallas as pl
from jax.experimental.pallas import tpu as pltpu
from jax.sharding import PartitionSpec as P

MESH = pl.DeviceIdType.MESH
LAG = 3
f32, bf16 = jnp.float32, jnp.bfloat16


def ring_offset(k, size):
    steps = size // 2 - (k + 1) // 2
    return steps * ((k % 2) * 2 - 1)


def ring_to(place, k, size):
    return (place + size + ring_offset(k, size)) % size


def ring_from(place, k, size):
    return (place + size - ring_offset(k, size)) % size


def dot(a, b, contract):
    return lax.dot_general(a, b, ((contract[:1], contract[1:]), ((), ())), preferred_element_type=f32)


def split_dot(a, b):
    high = b.astype(bf16)
    low = (b - high.astype(f32)).astype(bf16)
    return dot(a, high, (1, 0)) + dot(a, low, (1, 0))


def layer_kernel(
    wide, narrow,
    feat_ref, weight_ref, bias_ref, cls_ref, tiles_hbm, col_ref, count_ref, prev_ref, perm_ref, labels_ref,
    next_ref, loss_ref, grad_ref,
    tiles, ft, sbuf, srecv, xbuf, xrecv, zbuf, zrecv, own, gbuf, run,
    pack, unpack, cxbuf, cxrecv, cybuf, cyrecv, cpad,
    tile_sem, fy_s, fy_r, fx_s, fx_r, s_s, s_r, x_s, x_r, z_s, z_r,
    gz_s, gz_r, gx_s, gx_r, gs_s, gs_r, cx_s, cx_r, cy_s, cy_r, a_s, a_r,
):
    Y, Z = wide // 2, narrow // 4
    w, n = lax.axis_index("wide"), lax.axis_index("narrow")
    xl, y = w // Y, w % Y
    xh, z, c = n // (2 * Z), (n // 2) % Z, n % 2

    def nid(xh_, z_, c_):
        return (xh_ * Z + z_) * 2 + c_

    def rcopy(src, dst, ss, rs, dev):
        return pltpu.make_async_remote_copy(
            src_ref=src, dst_ref=dst, send_sem=ss, recv_sem=rs, device_id=dev, device_id_type=MESH
        )

    x_dev = (w, nid(1 - xh, z, c))
    s_dev = (w, nid(xh, z, 1 - c))
    xl_dev = ((1 - xl) * Y + y, n)

    def z_dev(k):
        return (w, nid(xh, ring_to(z, k, Z), c))

    def y_dev(k):
        return (xl * Y + ring_to(y, k, Y), n)

    barrier = pltpu.get_barrier_semaphore()
    for d in range(1, wide):
        pl.semaphore_signal(barrier, inc=1, device_id=((w + d) % wide, n), device_id_type=MESH)
    for k in range(Z - 1):
        pl.semaphore_signal(barrier, inc=1, device_id=z_dev(k), device_id_type=MESH)
    pl.semaphore_signal(barrier, inc=1, device_id=x_dev, device_id_type=MESH)
    pl.semaphore_signal(barrier, inc=1, device_id=s_dev, device_id_type=MESH)

    tile_copy = pltpu.make_async_copy(tiles_hbm, tiles, tile_sem)
    tile_copy.start()
    ft[w] = feat_ref[...].astype(f32).T.astype(bf16)
    ft[wide] = jnp.zeros_like(ft[wide])
    run[0] = jnp.zeros_like(run[0])

    pl.semaphore_wait(barrier, wide - 1 + Z - 1 + 2)

    def fy(k, slot):
        return rcopy(ft.at[slot], ft.at[slot], fy_s.at[k], fy_r.at[k], y_dev(k))

    def fx(k, slot):
        return rcopy(ft.at[slot], ft.at[slot], fx_s.at[k], fx_r.at[k], xl_dev)

    fx(Y - 1, w).start()
    for k in range(Y - 1):
        fy(k, w).start()

    weight = weight_ref[...]
    weight_t = weight.astype(f32).T.astype(bf16)
    bias = jnp.broadcast_to(bias_ref[...], (perm_ref.shape[1], bias_ref.shape[1])).T
    classes = cls_ref.shape[1]
    cpad[...] = jnp.zeros_like(cpad)
    cpad[:, :classes] = cls_ref[...]

    nodes = perm_ref.shape[1]
    slots = unpack.shape[0] // wide
    perm_row = jnp.broadcast_to(perm_ref[...], (nodes, nodes))
    perm_col = perm_row.astype(f32).T.astype(jnp.int32)
    dest_row, dest_col = perm_row // nodes, perm_col // nodes
    sub = lax.broadcasted_iota(jnp.int32, (nodes, nodes), 0)
    lane = lax.broadcasted_iota(jnp.int32, (nodes, nodes), 1)
    rank = jnp.sum(((dest_row == dest_col) & (sub < lane)).astype(jnp.int32), axis=0, keepdims=True)
    place_row = perm_ref[...] // nodes * slots + rank
    chosen = (
        lax.broadcasted_iota(jnp.int32, (wide * slots, nodes), 0) == place_row
    ).astype(f32).astype(bf16)
    where_to = (perm_col - dest_col * nodes == lane).astype(f32).astype(bf16)
    hidden = bias_ref.shape[1]
    pack[:, hidden:] = dot(chosen, where_to, (1, 0)).astype(bf16)

    for k in range(Y - 1):
        slot = xl * Y + ring_from(y, k, Y)
        fy(k, slot).wait_recv()
        fx(k, slot).start()
    tile_copy.wait()
    for k in range(Y):
        fx(k, (1 - xl) * Y + ring_from(y, k, Y)).wait_recv()

    def aggregate(b):
        first = col_ref[2 * b]
        second = jnp.where(count_ref[b] > 1, col_ref[2 * b + 1], wide)
        left = jnp.concatenate([ft[first], ft[second]], axis=1)
        right = jnp.concatenate([tiles[2 * b], tiles[2 * b + 1]], axis=1)
        return dot(left, right, (1, 1))

    def s_copy(g, k):
        return rcopy(sbuf.at[g, k], srecv.at[g, k], s_s.at[g, k], s_r.at[g, k], s_dev)

    def x_copy(k):
        return rcopy(xbuf.at[k], xrecv.at[k], x_s.at[k], x_r.at[k], x_dev)

    def z_copy(k):
        return rcopy(zbuf.at[k], zrecv.at[k], z_s.at[k], z_r.at[k], z_dev(k))

    @pl.loop(0, Z)
    def _(k):
        sbuf[0, k] = aggregate(nid(1 - xh, ring_to(z, k, Z), 1 - c)).astype(bf16)
        s_copy(0, k).start()

    @pl.loop(0, Z)
    def _(k):
        part = aggregate(nid(1 - xh, ring_to(z, k, Z), c))
        s_copy(0, k).wait_recv()
        xbuf[k] = (part + srecv[0, k].astype(f32)).astype(bf16)
        x_copy(k).start()

    @pl.loop(0, Z)
    def _(k):
        sbuf[1, k] = aggregate(nid(xh, ring_to(z, k, Z), 1 - c)).astype(bf16)
        s_copy(1, k).start()

    @pl.loop(0, Z)
    def _(k):
        part = aggregate(nid(xh, ring_to(z, k, Z), c))
        s_copy(1, k).wait_recv()
        own[k] = part + srecv[1, k].astype(f32)

    @pl.loop(0, Z - 1)
    def _(k):
        x_copy(k).wait_recv()
        zbuf[k] = (own[k] + xrecv[k].astype(f32)).astype(bf16)
        z_copy(k).start()

    x_copy(Z - 1).wait_recv()
    total = own[Z - 1] + xrecv[Z - 1].astype(f32)
    for k in range(Z - 1):
        z_copy(k).wait_recv()
        total = total + zrecv[k].astype(f32)

    hidden_pre = split_dot(weight_t, total) + bias
    gate_value = jax.nn.sigmoid(hidden_pre)
    activated = (hidden_pre * gate_value).astype(bf16)
    class_id = lax.broadcasted_iota(jnp.int32, (cpad.shape[1], nodes), 0)
    logits = dot(cpad[...].astype(f32).T.astype(bf16), activated, (1, 0))
    logits = jnp.where(class_id < classes, logits, -jnp.inf)
    top_score = jnp.max(logits, axis=0, keepdims=True)
    shifted = jnp.exp(logits - top_score)
    exp_total = jnp.sum(shifted, axis=0, keepdims=True)
    target = class_id == labels_ref[...]
    grad_logits = shifted / exp_total - target.astype(f32)
    grad_act = split_dot(cpad[...], grad_logits)
    grad_pre = (grad_act * gate_value * (1.0 + hidden_pre * (1.0 - gate_value))).astype(bf16)
    gbuf[n] = dot(weight, grad_pre, (1, 0)).astype(bf16)

    def gz(k, slot):
        return rcopy(gbuf.at[slot], gbuf.at[slot], gz_s.at[k], gz_r.at[k], z_dev(k))

    def gx(k, slot):
        return rcopy(gbuf.at[slot], gbuf.at[slot], gx_s.at[k], gx_r.at[k], x_dev)

    def gs(g, k, slot):
        return rcopy(gbuf.at[slot], gbuf.at[slot], gs_s.at[g, k], gs_r.at[g, k], s_dev)

    for k in range(Z - 2, -1, -1):
        gz(k, n).start()

    pack[:, :hidden] = dot(chosen, activated, (1, 1)).astype(bf16)

    def a_copy(d, src, dst):
        return rcopy(
            pack.at[pl.ds(src * slots, slots)], unpack.at[pl.ds(dst * slots, slots)],
            a_s.at[d], a_r.at[d], ((w + d) % wide, n),
        )

    for d in range(1, wide):
        a_copy(d, (w + d) % wide, w).start()
    mine = pl.ds(pl.multiple_of(w * slots, slots), slots)
    unpack[mine, :] = pack[mine, :]
    picked = jnp.sum(jnp.where(target, logits, 0.0), axis=0, keepdims=True)
    loss_ref[...] = top_score + jnp.log(exp_total) - picked

    def spread(b):
        right = jnp.concatenate([tiles[2 * b], tiles[2 * b + 1]], axis=1)
        part = dot(gbuf[b], right, (1, 0))
        for t in range(2):
            run[2 * b + t + 1] = part[:, t * nodes : (t + 1) * nodes] + run[prev_ref[2 * b + t]]

    @pl.loop(0, Z + LAG + 1)
    def _(j):
        @pl.when(j < Z)
        def _():
            k = Z - 1 - j
            slot = nid(xh, ring_from(z, k, Z), c)

            @pl.when(j > 0)
            def _():
                gz(k, slot).wait_recv()

            gx(k, slot).start()
            gs(0, k, slot).start()
            spread(slot)

        @pl.when((j >= LAG) & (j < Z + LAG))
        def _():
            k = Z - 1 - j + LAG
            slot = nid(1 - xh, ring_from(z, k, Z), c)
            gx(k, slot).wait_recv()
            gs(1, k, slot).start()
            spread(slot)

        @pl.when((j >= 1) & (j < Z + 1))
        def _():
            k = Z - j
            slot = nid(xh, ring_from(z, k, Z), 1 - c)
            gs(0, k, slot).wait_recv()
            spread(slot)

        @pl.when(j >= LAG + 1)
        def _():
            k = Z - j + LAG
            slot = nid(1 - xh, ring_from(z, k, Z), 1 - c)
            gs(1, k, slot).wait_recv()
            spread(slot)

    last = narrow * 2

    def cx(k):
        return rcopy(cxbuf.at[k], cxrecv.at[k], cx_s.at[k], cx_r.at[k], xl_dev)

    def cy(k):
        return rcopy(cybuf.at[k], cyrecv.at[k], cy_s.at[k], cy_r.at[k], y_dev(k))

    for k in range(Y):
        cxbuf[k] = run[prev_ref[last + (1 - xl) * Y + ring_to(y, k, Y)]].astype(bf16)
        cx(k).start()

    for d in range(1, wide):
        a_copy(d, w, (w + wide - d) % wide).wait_recv()
    next_ref[...] = dot(unpack[:, hidden:], unpack[:, :hidden], (0, 0)).astype(bf16)

    for k in range(Y):
        part = run[prev_ref[last + xl * Y + ring_to(y, k, Y)]]
        cx(k).wait_recv()
        part = part + cxrecv[k].astype(f32)
        if k < Y - 1:
            cybuf[k] = part.astype(bf16)
            cy(k).start()
    for k in range(Y - 1):
        cy(k).wait_recv()
        part = part + cyrecv[k].astype(f32)
    grad_ref[...] = part.T

    for k in range(Y):
        fx(k, w).wait_send()
        cx(k).wait_send()
        if k < Y - 1:
            fy(k, w).wait_send()
            cy(k).wait_send()
    for d in range(1, wide):
        a_copy(d, (w + d) % wide, w).wait_send()

    @pl.loop(0, Z)
    def _(k):
        s_copy(0, k).wait_send()
        s_copy(1, k).wait_send()
        x_copy(k).wait_send()
        gx(k, n).wait_send()
        gs(0, k, n).wait_send()
        gs(1, k, n).wait_send()

    @pl.loop(0, Z - 1)
    def _(k):
        z_copy(k).wait_send()
        gz(k, n).wait_send()


def chain_table(columns, counts, wide, narrow):
    size = narrow // 4
    n = lax.axis_index("narrow")
    slot = lax.iota(jnp.int32, narrow * 2)
    b = slot // 2
    xb, zb, cb = b // (2 * size), (b // 2) % size, b % 2
    far = ((n // 2) % size - zb + size) % size
    half = size // 2
    k = jnp.where(far > half, 2 * (far - half), jnp.where(far == half, 0, 2 * (half - far) - 1))
    other_x, other_c = xb != n // (2 * size), cb != n % 2
    step = size - 1 - k + jnp.where(other_x, LAG, 0) + jnp.where(other_c, 1, 0)
    kind = jnp.where(other_x, 1, 0) + jnp.where(other_c, 2, 0)
    when = step * 4 + kind
    column = jnp.where(slot % 2 < counts[b], columns, wide)
    key = when * 256 + slot + 1
    ask_column = jnp.concatenate([column, jnp.arange(wide, dtype=jnp.int32)])
    ask_before = jnp.concatenate([when * 256, jnp.full((wide,), 1 << 30, jnp.int32)])
    fits = (column[None, :] == ask_column[:, None]) & (key[None, :] < ask_before[:, None])
    return jnp.max(jnp.where(fits, key[None, :], 0), axis=1) % 256


def per_device(
    wide, narrow, features, in_weight, hidden_bias, classifier, adjacency_tiles, tile_col, tile_count, node_perm, labels
):
    nodes, f_in = features.shape[1], features.shape[2]
    hidden = in_weight.shape[1]
    tile = adjacency_tiles.shape[3]
    Y, Z = wide // 2, narrow // 4
    columns = tile_col.reshape(-1)
    counts = tile_count.reshape(-1)
    table = chain_table(columns, counts, wide, narrow)
    padded = -(-classifier.shape[1] // 128) * 128
    slots = 16
    block = (f_in, tile)
    vmem = pl.BlockSpec(memory_space=pltpu.VMEM)
    smem = pl.BlockSpec(memory_space=pltpu.SMEM)
    dma = pltpu.SemaphoreType.DMA
    next_rows, node_loss, input_grad = pl.pallas_call(
        functools.partial(layer_kernel, wide, narrow),
        out_shape=(
            jax.ShapeDtypeStruct((nodes, hidden), bf16),
            jax.ShapeDtypeStruct((1, nodes), f32),
            jax.ShapeDtypeStruct((nodes, f_in), f32),
        ),
        in_specs=[vmem, vmem, vmem, vmem, pl.BlockSpec(memory_space=pl.ANY), smem, smem, smem, vmem, vmem],
        out_specs=(vmem, vmem, vmem),
        scratch_shapes=[
            pltpu.VMEM((narrow * 2, tile, tile), bf16),
            pltpu.VMEM((wide + 1,) + block, bf16),
            pltpu.VMEM((2, Z) + block, bf16),
            pltpu.VMEM((2, Z) + block, bf16),
            pltpu.VMEM((Z,) + block, bf16),
            pltpu.VMEM((Z,) + block, bf16),
            pltpu.VMEM((Z - 1,) + block, bf16),
            pltpu.VMEM((Z - 1,) + block, bf16),
            pltpu.VMEM((Z,) + block, f32),
            pltpu.VMEM((narrow,) + block, bf16),
            pltpu.VMEM((narrow * 2 + 1,) + block, f32),
            pltpu.VMEM((wide * slots, hidden + nodes), bf16),
            pltpu.VMEM((wide * slots, hidden + nodes), bf16),
            pltpu.VMEM((Y,) + block, bf16),
            pltpu.VMEM((Y,) + block, bf16),
            pltpu.VMEM((Y - 1,) + block, bf16),
            pltpu.VMEM((Y - 1,) + block, bf16),
            pltpu.VMEM((hidden, padded), bf16),
            dma,
            dma((Y - 1,)), dma((Y - 1,)), dma((Y,)), dma((Y,)),
            dma((2, Z)), dma((2, Z)), dma((Z,)), dma((Z,)), dma((Z - 1,)), dma((Z - 1,)),
            dma((Z - 1,)), dma((Z - 1,)), dma((Z,)), dma((Z,)), dma((2, Z)), dma((2, Z)),
            dma((Y,)), dma((Y,)), dma((Y - 1,)), dma((Y - 1,)), dma((wide,)), dma((wide,)),
        ],
        compiler_params=pltpu.CompilerParams(
            collective_id=0, has_side_effects=True, vmem_limit_bytes=48 * 2**20
        ),
        name="layer",
    )(
        features.reshape(nodes, f_in), in_weight, hidden_bias.reshape(1, hidden), classifier,
        adjacency_tiles.reshape(-1, tile, tile), columns, counts, table, node_perm, labels.reshape(1, nodes),
    )
    return next_rows.reshape(1, nodes, hidden), node_loss.reshape(nodes), input_grad.reshape(1, nodes, f_in)


def solution(mesh):
    in_specs = (
        P("narrow", "wide", None),
        P(),
        P(),
        P(),
        P("wide", "narrow", None, None, None),
        P("wide", "narrow", None),
        P("wide", "narrow"),
        P("narrow", "wide"),
        P(("wide", "narrow")),
    )
    out_specs = (P("narrow", "wide", None), P(("wide", "narrow")), P("narrow", "wide", None))
    return jax.shard_map(
        functools.partial(per_device, mesh.shape["wide"], mesh.shape["narrow"]),
        mesh=mesh, in_specs=in_specs, out_specs=out_specs, check_vma=False,
    )
```

```python
import functools

import jax
import jax.numpy as jnp
from jax import lax
from jax.experimental import pallas as pl
from jax.experimental.pallas import tpu as pltpu
from jax.sharding import PartitionSpec as P

MESH = pl.DeviceIdType.MESH
RELAY = 3
INWARD = (6, 5, -5, 4, -4, 3, -3, 2, -2, 1, -1, 0)
FAR, NEAR = INWARD[:5], INWARD[5:]
ARRIVALS = (
    ("own", 0), ("own", 3), ("own", -3), ("own", 1), ("own", -1), ("x", 0), ("own", 2), ("own", -2),
    ("x", 3), ("x", -3), ("x", 1), ("x", -1), ("own", 4), ("own", -4), ("own", 5), ("own", -5), ("own", 6),
    ("x", 2), ("x", -2), ("other", 4), ("other", -4), ("other", 5), ("other", -5), ("other", 6),
)
SIBLING_LAG = 2


def spread_order():
    order = []
    for i in range(len(ARRIVALS) + SIBLING_LAG):
        for j, sibling in ((i, 0), (i - SIBLING_LAG, 1)):
            if 0 <= j < len(ARRIVALS):
                kind, offset = ARRIVALS[j]
                order.append((int(kind != "own"), sibling, offset))
    return order


f32, bf16 = jnp.float32, jnp.bfloat16


def ring_offset(k, size):
    steps = size // 2 - (k + 1) // 2
    return steps * ((k % 2) * 2 - 1)


def ring_step(place, offset, size):
    moved = place + offset
    if offset > 0:
        return jnp.where(moved >= size, moved - size, moved)
    return jnp.where(moved < 0, moved + size, moved) if offset else place


def ring_to(place, k, size):
    return ring_step(place, ring_offset(k, size), size)


def ring_from(place, k, size):
    return ring_step(place, -ring_offset(k, size), size)


def dot(a, b, contract):
    return lax.dot_general(a, b, ((contract[:1], contract[1:]), ((), ())), preferred_element_type=f32)


def split_dot(a, b):
    high = b.astype(bf16)
    low = (b - high.astype(f32)).astype(bf16)
    return dot(a, high, (1, 0)) + dot(a, low, (1, 0))


def turned(row, size):
    return jnp.broadcast_to(row.astype(f32), (size, size)).T.astype(jnp.int32)


def layer_kernel(
    wide, narrow,
    feat_hbm, weight_hbm, bias_hbm, cls_hbm, tiles_hbm, cols_hbm, counts_hbm, perm_hbm, labels_hbm,
    next_ref, loss_ref, grad_ref,
    feat, weight, bias, cls, tiles, cols, counts, perm, labels, table_v, table,
    ft, sbuf, srecv, fbuf, frecv, xbuf, xrecv, zbuf, zrecv, own, gbuf, run,
    pack, unpack, cxbuf, cxrecv, cybuf, cyrecv, cpad,
    in_sem, table_sem, fy_s, fy_r, fx_s, fx_r, s_s, s_r, f_s, f_r, x_s, x_r, z_s, z_r,
    gz_s, gz_r, gx_s, gx_r, gs_s, gs_r, cx_s, cx_r, cy_s, cy_r, a_s, a_r,
):
    Y, Z = wide // 2, narrow // 4
    w, n = lax.axis_index("wide"), lax.axis_index("narrow")
    xl, y = w // Y, w % Y
    xh, z, c = n // (2 * Z), (n // 2) % Z, n % 2

    def nid(xh_, z_, c_):
        return (xh_ * Z + z_) * 2 + c_

    def rcopy(src, dst, ss, rs, dev):
        return pltpu.make_async_remote_copy(
            src_ref=src, dst_ref=dst, send_sem=ss, recv_sem=rs, device_id=dev, device_id_type=MESH
        )

    x_dev = (w, nid(1 - xh, z, c))
    s_dev = (w, nid(xh, z, 1 - c))
    xl_dev = ((1 - xl) * Y + y, n)

    sign = 1 - 2 * c

    def zat(offset, facing=1):
        moved = z + sign * (facing * offset)
        return jnp.where(moved < 0, moved + Z, jnp.where(moved >= Z, moved - Z, moved))

    def z_dev(offset):
        return (w, nid(xh, zat(offset), c))

    def y_dev(k):
        return (xl * Y + ring_to(y, k, Y), n)

    def w_dev(d):
        return (ring_step(w, d, wide), n)

    barrier = pltpu.get_barrier_semaphore()
    partners = [w_dev(d) for d in range(1, wide)] + [z_dev(o) for o in (1, -1, 2, -2, 3, -3)] + [x_dev, s_dev]
    for partner in partners:
        pl.semaphore_signal(barrier, inc=1, device_id=partner, device_id_type=MESH)

    inputs = [
        pltpu.make_async_copy(src, dst, in_sem.at[i])
        for i, (src, dst) in enumerate((
            (feat_hbm, feat), (cols_hbm, cols), (counts_hbm, counts), (perm_hbm, perm), (weight_hbm, weight),
            (bias_hbm, bias), (cls_hbm, cls), (labels_hbm, labels), (tiles_hbm, tiles),
        ))
    ]
    for copy in inputs:
        copy.start()
    run[0] = jnp.zeros_like(run[0])
    ft[wide] = jnp.zeros_like(ft[wide])
    table_v[...] = jnp.full(table_v.shape, -1, jnp.int32)
    cpad[...] = jnp.zeros_like(cpad)
    inputs[0].wait()
    ft[w] = feat[...].astype(f32).T.astype(bf16)

    for copy in inputs[1:4]:
        copy.wait()
    nodes = perm.shape[1]
    table_v[0:2, :narrow] = cols[...]
    table_v[2:3, :narrow] = counts[...]
    lane_row = lax.broadcasted_iota(jnp.int32, (1, nodes), 1)
    in_upper = (lane_row >= 2 * Z).astype(jnp.int32)
    in_half = lane_row - 2 * Z * in_upper
    far = ((in_half >> 1) - z) * (1 - 2 * (in_half & 1))
    far = jnp.where(far < 0, far + Z, far)
    other_x, other_c = jnp.abs(in_upper - xh), jnp.abs((in_half & 1) - c)
    kind = (other_x * 2 + other_c) * Z + far
    when = jnp.zeros_like(far)
    for turn, (column_, core, offset) in enumerate(spread_order()):
        when = jnp.where(kind == (column_ * 2 + core) * Z + offset % Z, turn, when)
    column = [table_v[0:1, :], jnp.where(table_v[2:3, :] > 1, table_v[1:2, :], jnp.where(lane_row < narrow, wide, -1))]
    key = [when * 256 + 2 * lane_row + 1 + t for t in range(2)]
    column_down = [turned(row, nodes) for row in column]
    key_down = [turned(row, nodes) for row in key]
    for t in range(2):
        fits = [
            jnp.where((column_down[u] == column[t]) & (key_down[u] < when * 256), key_down[u], 0) for u in range(2)
        ]
        table_v[2 + t : 3 + t, :] = jnp.max(jnp.maximum(fits[0], fits[1]), axis=0, keepdims=True) & 255
    fits = [jnp.where(column_down[u] == lane_row, key_down[u], 0) for u in range(2)]
    table_v[4:5, :] = jnp.max(jnp.maximum(fits[0], fits[1]), axis=0, keepdims=True) & 255
    table_v[1:2, :] = column[1]
    table_copy = pltpu.make_async_copy(table_v, table, table_sem)
    table_copy.start()

    pl.semaphore_wait(barrier, len(partners))

    def fy(k, slot):
        return rcopy(ft.at[slot], ft.at[slot], fy_s.at[k], fy_r.at[k], y_dev(k))

    def fx(k, slot):
        return rcopy(ft.at[slot], ft.at[slot], fx_s.at[k], fx_r.at[k], xl_dev)

    fx(Y - 1, w).start()
    for k in range(Y - 1):
        fy(k, w).start()

    slots = unpack.shape[0] // wide
    hidden = bias.shape[1]
    perm_row = perm[...]
    shift = nodes.bit_length() - 1
    dest_row, perm_col = perm_row >> shift, turned(perm_row, nodes)
    dest_col = perm_col >> shift
    sub = lax.broadcasted_iota(jnp.int32, (nodes, nodes), 0)
    lane = lax.broadcasted_iota(jnp.int32, (nodes, nodes), 1)
    rank = jnp.sum(((dest_row == dest_col) & (sub < lane)).astype(jnp.int32), axis=0, keepdims=True)
    place_row = dest_row * slots + rank
    chosen = (
        lax.broadcasted_iota(jnp.int32, (wide * slots, nodes), 0) == place_row
    ).astype(f32).astype(bf16)
    where_to = (perm_col - dest_col * nodes == lane).astype(f32).astype(bf16)
    pack[:, hidden:] = dot(chosen, where_to, (1, 0)).astype(bf16)

    for copy in inputs[4:8]:
        copy.wait()
    weight_t = weight[...].astype(f32).T.astype(bf16)
    bias_t = jnp.broadcast_to(bias[...], (nodes, hidden)).T
    classes = cls.shape[0]
    cpad[:classes, :] = cls[...]
    cls_t = cpad[...].astype(f32).T.astype(bf16)

    for k in range(Y - 1):
        slot = xl * Y + ring_from(y, k, Y)
        fy(k, slot).wait_recv()
        fx(k, slot).start()
    table_copy.wait()
    inputs[8].wait()
    for k in range(Y):
        fx(k, (1 - xl) * Y + ring_from(y, k, Y)).wait_recv()

    def aggregate(b):
        left = jnp.concatenate([ft[table[0, b]], ft[table[1, b]]], axis=1)
        right = jnp.concatenate([tiles[2 * b], tiles[2 * b + 1]], axis=1)
        return dot(left, right, (1, 1))

    def s_copy(g, k):
        return rcopy(sbuf.at[g, k], srecv.at[g, k], s_s.at[g, k], s_r.at[g, k], s_dev)

    def x_copy(k):
        return rcopy(xbuf.at[k], xrecv.at[k], x_s.at[k], x_r.at[k], x_dev)

    def far_copy(g, k):
        relay = FAR[k] - RELAY if FAR[k] > 0 else FAR[k] + RELAY
        return rcopy(fbuf.at[g, k], frecv.at[g, k], f_s.at[g, k], f_r.at[g, k], z_dev(relay))

    def z_copy(k):
        return rcopy(zbuf.at[k], zrecv.at[k], z_s.at[k], z_r.at[k], z_dev(NEAR[k]))

    columns = (1 - xh, xh)

    def begin(g, k):
        sbuf[g, k] = aggregate(nid(columns[g], zat(INWARD[k], -1), 1 - c)).astype(bf16)
        s_copy(g, k).start()
        own[g, k] = aggregate(nid(columns[g], zat(INWARD[k]), c))

    def chip_sum(g, k):
        s_copy(g, k).wait_recv()
        return own[g, k] + srecv[g, k].astype(f32)

    def add_far(g, k, part):
        for u in range(5):
            if FAR[u] * NEAR[k] > 0:
                far_copy(g, u).wait_recv()
                part = part + frecv[g, u].astype(f32)
        return part

    for g in range(2):
        for k in range(5):
            begin(g, k)
    for k in range(5, Z):
        begin(0, k)
        if k < 10:
            fbuf[0, k - 5] = chip_sum(0, k - 5).astype(bf16)
            far_copy(0, k - 5).start()
    for k in range(5, Z):
        begin(1, k)
        if k < 10:
            fbuf[1, k - 5] = chip_sum(1, k - 5).astype(bf16)
            far_copy(1, k - 5).start()
    for k in range(2, 7):
        xbuf[k] = chip_sum(0, k + 5).astype(bf16)
        x_copy(k).start()
    for k in range(2):
        xbuf[k] = add_far(0, k, chip_sum(0, k + 5)).astype(bf16)
        x_copy(k).start()
    for k in range(2, 6):
        part = chip_sum(1, k + 5)
        x_copy(k).wait_recv()
        zbuf[k] = (part + xrecv[k].astype(f32)).astype(bf16)
        z_copy(k).start()
    for k in range(2):
        part = add_far(1, k, chip_sum(1, k + 5))
        x_copy(k).wait_recv()
        zbuf[k] = (part + xrecv[k].astype(f32)).astype(bf16)
        z_copy(k).start()
    total = chip_sum(1, Z - 1)
    x_copy(6).wait_recv()
    total = total + xrecv[6].astype(f32)
    for k in (2, 3, 4, 5, 0, 1):
        z_copy(k).wait_recv()
        total = total + zrecv[k].astype(f32)

    def wait_forward():
        for k in range(Y):
            fx(k, w).wait_send()
            if k < Y - 1:
                fy(k, w).wait_send()
        for k in range(Z):
            s_copy(0, k).wait_send()
            s_copy(1, k).wait_send()
        for k in range(5):
            far_copy(0, k).wait_send()
            far_copy(1, k).wait_send()
        for k in range(7):
            x_copy(k).wait_send()
        for k in range(6):
            z_copy(k).wait_send()


    hidden_pre = split_dot(weight_t, total) + bias_t
    gate_value = jax.nn.sigmoid(hidden_pre)
    activated = (hidden_pre * gate_value).astype(bf16)
    class_id = lax.broadcasted_iota(jnp.int32, (cpad.shape[0], nodes), 0)
    logits = dot(cpad[...], activated, (1, 0))
    logits = jnp.where(class_id < classes, logits, -jnp.inf)
    top_score = jnp.max(logits, axis=0, keepdims=True)
    shifted = jnp.exp(logits - top_score)
    exp_total = jnp.sum(shifted, axis=0, keepdims=True)
    target = class_id == labels[...]
    grad_logits = shifted / exp_total - target.astype(f32)
    grad_act = split_dot(cls_t, grad_logits)
    grad_pre = (grad_act * gate_value * (1.0 + hidden_pre * (1.0 - gate_value))).astype(bf16)
    gbuf[n] = dot(weight[...], grad_pre, (1, 0)).astype(bf16)

    def gz(g, offset, slot, towards):
        k = INWARD.index(offset)
        return rcopy(gbuf.at[slot], gbuf.at[slot], gz_s.at[g, k], gz_r.at[g, k], z_dev(towards))

    def gx(offset, slot):
        k = INWARD.index(offset)
        return rcopy(gbuf.at[slot], gbuf.at[slot], gx_s.at[k], gx_r.at[k], x_dev)

    def gs(g, offset, slot):
        k = INWARD.index(offset)
        return rcopy(gbuf.at[slot], gbuf.at[slot], gs_s.at[g, k], gs_r.at[g, k], s_dev)

    def pass_on(g, offset, slot):
        if offset == -RELAY:
            for further, seen_at in ((3, 6), (2, -5), (1, -4)):
                gz(g, seen_at, slot, further).start()
        if offset == RELAY:
            for further, seen_at in ((-2, 5), (-1, 4)):
                gz(g, seen_at, slot, further).start()

    gx(0, n).start()
    for offset in (3, -3, 1, -1, 2, -2):
        gz(0, -offset, n, offset).start()
    gs(0, 0, n).start()

    pack[:, :hidden] = dot(chosen, activated, (1, 1)).astype(bf16)

    def a_copy(d, src, dst):
        return rcopy(
            pack.at[pl.ds(src * slots, slots)], unpack.at[pl.ds(dst * slots, slots)],
            a_s.at[d], a_r.at[d], w_dev(d),
        )

    for d in range(1, wide):
        a_copy(d, ring_step(w, d, wide), w).start()
    mine = pl.ds(pl.multiple_of(w * slots, slots), slots)
    unpack[mine, :] = pack[mine, :]
    picked = jnp.sum(jnp.where(target, logits, 0.0), axis=0, keepdims=True)
    loss_ref[...] = top_score + jnp.log(exp_total) - picked

    def spread(b):
        right = jnp.concatenate([tiles[2 * b], tiles[2 * b + 1]], axis=1)
        part = dot(gbuf[b], right, (1, 0))
        for t in range(2):
            run[2 * b + t + 1] = part[:, t * nodes : (t + 1) * nodes] + run[table[2 + t, b]]

    for i in range(len(ARRIVALS) + SIBLING_LAG):
        ready = []
        if i < len(ARRIVALS):
            kind, offset = ARRIVALS[i]
            g = int(kind != "own")
            slot = nid(xh if g == 0 else 1 - xh, zat(offset), c)
            if kind == "x":
                gx(offset, slot).wait_recv()
                pass_on(1, offset, slot)
                gs(1, offset, slot).start()
            elif offset:
                gz(g, offset, slot, 1).wait_recv()
                if kind == "own":
                    pass_on(0, offset, slot)
                    if offset in NEAR:
                        gx(offset, slot).start()
                gs(g, offset, slot).start()
            ready.append(slot)
        if i >= SIBLING_LAG:
            kind, offset = ARRIVALS[i - SIBLING_LAG]
            g = int(kind != "own")
            slot = nid(xh if g == 0 else 1 - xh, zat(offset, -1), 1 - c)
            gs(g, offset, slot).wait_recv()
            ready.append(slot)
        for slot in ready:
            spread(slot)

    def wait_backward():
        for d in range(1, wide):
            a_copy(d, ring_step(w, d, wide), w).wait_send()
        for offset in INWARD:
            gs(0, offset, n).wait_send()
            gs(1, offset, n).wait_send()
            if offset in NEAR:
                gx(offset, n).wait_send()
            else:
                gz(1, offset, n, 1).wait_send()
            if offset:
                gz(0, offset, n, 1).wait_send()

    def place():
        for d in range(1, wide):
            a_copy(d, w, ring_step(w, -d, wide)).wait_recv()
        next_ref[...] = dot(unpack[:, hidden:], unpack[:, :hidden], (0, 0)).astype(bf16)


    def cx(k):
        return rcopy(cxbuf.at[k], cxrecv.at[k], cx_s.at[k], cx_r.at[k], xl_dev)

    def cy(k):
        return rcopy(cybuf.at[k], cyrecv.at[k], cy_s.at[k], cy_r.at[k], y_dev(k))

    for k in range(Y):
        cxbuf[k] = run[table[4, (1 - xl) * Y + ring_to(y, k, Y)]].astype(bf16)
        cx(k).start()

    place()

    for k in range(Y):
        part = run[table[4, xl * Y + ring_to(y, k, Y)]]
        cx(k).wait_recv()
        part = part + cxrecv[k].astype(f32)
        if k < Y - 1:
            cybuf[k] = part.astype(bf16)
            cy(k).start()
    for k in range(Y - 1):
        cy(k).wait_recv()
        part = part + cyrecv[k].astype(f32)
    grad_ref[...] = part.T

    wait_forward()
    wait_backward()
    for k in range(Y):
        cx(k).wait_send()
        if k < Y - 1:
            cy(k).wait_send()


def per_device(
    wide, narrow, features, in_weight, hidden_bias, classifier, adjacency_tiles, tile_col, tile_count, node_perm, labels
):
    nodes, f_in = features.shape[1], features.shape[2]
    hidden = in_weight.shape[1]
    tile = adjacency_tiles.shape[3]
    Y, Z = wide // 2, narrow // 4
    padded = -(-classifier.shape[1] // 128) * 128
    slots = 16
    block = (f_in, tile)
    vmem = pl.BlockSpec(memory_space=pltpu.VMEM)
    hbm = pl.BlockSpec(memory_space=pltpu.HBM)
    dma = pltpu.SemaphoreType.DMA
    next_rows, node_loss, input_grad = pl.pallas_call(
        functools.partial(layer_kernel, wide, narrow),
        out_shape=(
            pltpu.VMEM((nodes, hidden), bf16),
            pltpu.VMEM((1, nodes), f32),
            pltpu.VMEM((nodes, f_in), f32),
        ),
        in_specs=[hbm] * 9,
        out_specs=(vmem, vmem, vmem),
        scratch_shapes=[
            pltpu.VMEM((nodes, f_in), bf16),
            pltpu.VMEM((f_in, hidden), bf16),
            pltpu.VMEM((1, hidden), f32),
            pltpu.VMEM(classifier.shape[::-1], bf16),
            pltpu.VMEM((narrow * 2, tile, tile), bf16),
            pltpu.VMEM((2, narrow), jnp.int32),
            pltpu.VMEM((1, narrow), jnp.int32),
            pltpu.VMEM((1, nodes), jnp.int32),
            pltpu.VMEM((1, nodes), jnp.int32),
            pltpu.VMEM((8, nodes), jnp.int32),
            pltpu.SMEM((8, nodes), jnp.int32),
            pltpu.VMEM((wide + 1,) + block, bf16),
            pltpu.VMEM((2, Z) + block, bf16),
            pltpu.VMEM((2, Z) + block, bf16),
            pltpu.VMEM((2, 5) + block, bf16),
            pltpu.VMEM((2, 5) + block, bf16),
            pltpu.VMEM((7,) + block, bf16),
            pltpu.VMEM((7,) + block, bf16),
            pltpu.VMEM((6,) + block, bf16),
            pltpu.VMEM((6,) + block, bf16),
            pltpu.VMEM((2, Z) + block, f32),
            pltpu.VMEM((narrow,) + block, bf16),
            pltpu.VMEM((narrow * 2 + 1,) + block, f32),
            pltpu.VMEM((wide * slots, hidden + nodes), bf16),
            pltpu.VMEM((wide * slots, hidden + nodes), bf16),
            pltpu.VMEM((Y,) + block, bf16),
            pltpu.VMEM((Y,) + block, bf16),
            pltpu.VMEM((Y - 1,) + block, bf16),
            pltpu.VMEM((Y - 1,) + block, bf16),
            pltpu.VMEM((padded, hidden), bf16),
            dma((9,)), dma,
            dma((Y - 1,)), dma((Y - 1,)), dma((Y,)), dma((Y,)),
            dma((2, Z)), dma((2, Z)), dma((2, 5)), dma((2, 5)), dma((7,)), dma((7,)), dma((6,)), dma((6,)),
            dma((2, Z)), dma((2, Z)), dma((Z,)), dma((Z,)), dma((2, Z)), dma((2, Z)),
            dma((Y,)), dma((Y,)), dma((Y - 1,)), dma((Y - 1,)), dma((wide,)), dma((wide,)),
        ],
        compiler_params=pltpu.CompilerParams(
            collective_id=0, has_side_effects=True, vmem_limit_bytes=61 * 2**20
        ),
        name="layer",
    )(
        features.reshape(nodes, f_in), in_weight, hidden_bias.reshape(1, hidden), classifier.T,
        adjacency_tiles.reshape(-1, tile, tile), tile_col.transpose(1, 2, 0).reshape(-1, narrow),
        tile_count.reshape(1, narrow), node_perm, labels.reshape(1, nodes),
    )
    return next_rows.reshape(1, nodes, hidden), node_loss.reshape(nodes), input_grad.reshape(1, nodes, f_in)


def solution(mesh):
    in_specs = (
        P("narrow", "wide", None),
        P(),
        P(),
        P(),
        P("wide", "narrow", None, None, None),
        P("wide", "narrow", None),
        P("wide", "narrow"),
        P("narrow", "wide"),
        P(("wide", "narrow")),
    )
    out_specs = (P("narrow", "wide", None), P(("wide", "narrow")), P("narrow", "wide", None))
    return jax.shard_map(
        functools.partial(per_device, mesh.shape["wide"], mesh.shape["narrow"]),
        mesh=mesh, in_specs=in_specs, out_specs=out_specs, check_vma=False,
    )
```

```python
import functools

import jax
import jax.numpy as jnp
from jax import lax
from jax.experimental import pallas as pl
from jax.experimental.pallas import tpu as pltpu
from jax.sharding import PartitionSpec as P

MESH = pl.DeviceIdType.MESH
RELAY = 3
INWARD = (6, 5, -5, 4, -4, 3, -3, 2, -2, 1, -1, 0)
FAR, NEAR = INWARD[:5], INWARD[5:]
Y_FAR, Y_NEAR = (4, 3, -3), (2, -2, 1, -1)
ARRIVALS = (
    ("own", 0), ("own", 3), ("own", -3), ("own", 1), ("own", -1), ("x", 0), ("own", 2), ("own", -2),
    ("x", 3), ("x", -3), ("x", 1), ("x", -1), ("own", 4), ("own", -4), ("own", 5), ("own", -5), ("own", 6),
    ("x", 2), ("x", -2), ("other", 4), ("other", -4), ("other", 5), ("other", -5), ("other", 6),
)
SIBLING_LAG = 6


def spread_order():
    order = []
    for i in range(len(ARRIVALS) + SIBLING_LAG):
        for j, sibling in ((i, 0), (i - SIBLING_LAG, 1)):
            if 0 <= j < len(ARRIVALS):
                kind, offset = ARRIVALS[j]
                order.append((int(kind != "own"), sibling, offset))
    return order


f32, bf16 = jnp.float32, jnp.bfloat16


def ring_offset(k, size):
    steps = size // 2 - (k + 1) // 2
    return steps * ((k % 2) * 2 - 1)


def ring_step(place, offset, size):
    moved = place + offset
    if offset > 0:
        return jnp.where(moved >= size, moved - size, moved)
    return jnp.where(moved < 0, moved + size, moved) if offset else place


def ring_to(place, k, size):
    return ring_step(place, ring_offset(k, size), size)


def ring_from(place, k, size):
    return ring_step(place, -ring_offset(k, size), size)


def dot(a, b, contract):
    return lax.dot_general(a, b, ((contract[:1], contract[1:]), ((), ())), preferred_element_type=f32)


def split_dot(a, b):
    high = b.astype(bf16)
    low = (b - high.astype(f32)).astype(bf16)
    return dot(a, high, (1, 0)) + dot(a, low, (1, 0))


def turned(row, size):
    return jnp.broadcast_to(row.astype(f32), (size, size)).T.astype(jnp.int32)


def layer_kernel(
    wide, narrow,
    feat_hbm, weight_hbm, bias_hbm, cls_hbm, tiles_hbm, cols_hbm, counts_hbm, perm_hbm, labels_hbm,
    next_ref, loss_ref, grad_ref,
    feat, weight, bias, cls, tiles, cols, counts, perm, labels, table_v, table,
    ft, sbuf, srecv, fbuf, frecv, xbuf, xrecv, zbuf, zrecv, own, gbuf, run,
    pack, unpack, cxbuf, cxrecv, cybuf, cyrecv, cnbuf, cnrecv, cpad,
    in_sem, table_sem, fy_s, fy_r, fx_s, fx_r, s_s, s_r, f_s, f_r, x_s, x_r, z_s, z_r,
    gz_s, gz_r, gx_s, gx_r, gs_s, gs_r, cx_s, cx_r, cy_s, cy_r, cn_s, cn_r, a_s, a_r,
):
    Y, Z = wide // 2, narrow // 4
    w, n = lax.axis_index("wide"), lax.axis_index("narrow")
    xl, y = w // Y, w % Y
    xh, z, c = n // (2 * Z), (n // 2) % Z, n % 2

    def nid(xh_, z_, c_):
        return (xh_ * Z + z_) * 2 + c_

    def rcopy(src, dst, ss, rs, dev):
        return pltpu.make_async_remote_copy(
            src_ref=src, dst_ref=dst, send_sem=ss, recv_sem=rs, device_id=dev, device_id_type=MESH
        )

    x_dev = (w, nid(1 - xh, z, c))
    s_dev = (w, nid(xh, z, 1 - c))
    xl_dev = ((1 - xl) * Y + y, n)

    sign = 1 - 2 * c

    def zat(offset, facing=1):
        moved = z + sign * (facing * offset)
        return jnp.where(moved < 0, moved + Z, jnp.where(moved >= Z, moved - Z, moved))

    def z_dev(offset):
        return (w, nid(xh, zat(offset), c))

    def y_dev(k):
        return (xl * Y + ring_to(y, k, Y), n)

    def w_dev(d):
        return (ring_step(w, d, wide), n)

    barrier = pltpu.get_barrier_semaphore()
    partners = [w_dev(d) for d in range(1, wide)] + [z_dev(o) for o in (1, -1, 2, -2, 3, -3)] + [x_dev, s_dev]
    for partner in partners:
        pl.semaphore_signal(barrier, inc=1, device_id=partner, device_id_type=MESH)

    inputs = [
        pltpu.make_async_copy(src, dst, in_sem.at[i])
        for i, (src, dst) in enumerate((
            (feat_hbm, feat), (cols_hbm, cols), (counts_hbm, counts), (perm_hbm, perm), (weight_hbm, weight),
            (bias_hbm, bias), (cls_hbm, cls), (labels_hbm, labels), (tiles_hbm, tiles),
        ))
    ]
    for copy in inputs:
        copy.start()
    run[0] = jnp.zeros_like(run[0])
    ft[wide] = jnp.zeros_like(ft[wide])
    table_v[...] = jnp.full(table_v.shape, -1, jnp.int32)
    cpad[...] = jnp.zeros_like(cpad)
    inputs[0].wait()
    ft[w] = feat[...].astype(f32).T.astype(bf16)

    for copy in inputs[1:4]:
        copy.wait()
    nodes = perm.shape[1]
    table_v[0:2, :narrow] = cols[...]
    table_v[2:3, :narrow] = counts[...]
    lane_row = lax.broadcasted_iota(jnp.int32, (1, nodes), 1)
    in_upper = (lane_row >= 2 * Z).astype(jnp.int32)
    in_half = lane_row - 2 * Z * in_upper
    far = ((in_half >> 1) - z) * (1 - 2 * (in_half & 1))
    far = jnp.where(far < 0, far + Z, far)
    other_x, other_c = jnp.abs(in_upper - xh), jnp.abs((in_half & 1) - c)
    kind = (other_x * 2 + other_c) * Z + far
    when = jnp.zeros_like(far)
    for turn, (column_, core, offset) in enumerate(spread_order()):
        when = jnp.where(kind == (column_ * 2 + core) * Z + offset % Z, turn, when)
    column = [table_v[0:1, :], jnp.where(table_v[2:3, :] > 1, table_v[1:2, :], jnp.where(lane_row < narrow, wide, -1))]
    key = [when * 256 + 2 * lane_row + 1 + t for t in range(2)]
    column_down = [turned(row, nodes) for row in column]
    key_down = [turned(row, nodes) for row in key]
    for t in range(2):
        fits = [
            jnp.where((column_down[u] == column[t]) & (key_down[u] < when * 256), key_down[u], 0) for u in range(2)
        ]
        table_v[2 + t : 3 + t, :] = jnp.max(jnp.maximum(fits[0], fits[1]), axis=0, keepdims=True) & 255
    fits = [jnp.where(column_down[u] == lane_row, key_down[u], 0) for u in range(2)]
    table_v[4:5, :] = jnp.max(jnp.maximum(fits[0], fits[1]), axis=0, keepdims=True) & 255
    table_v[1:2, :] = column[1]
    table_copy = pltpu.make_async_copy(table_v, table, table_sem)
    table_copy.start()

    pl.semaphore_wait(barrier, len(partners))

    def fy(k, slot):
        return rcopy(ft.at[slot], ft.at[slot], fy_s.at[k], fy_r.at[k], y_dev(k))

    def fx(k, slot):
        return rcopy(ft.at[slot], ft.at[slot], fx_s.at[k], fx_r.at[k], xl_dev)

    fx(Y - 1, w).start()
    for k in range(Y - 1):
        fy(k, w).start()

    slots = unpack.shape[0] // wide
    hidden = bias.shape[1]
    perm_row = perm[...]
    shift = nodes.bit_length() - 1
    dest_row, perm_col = perm_row >> shift, turned(perm_row, nodes)
    dest_col = perm_col >> shift
    sub = lax.broadcasted_iota(jnp.int32, (nodes, nodes), 0)
    lane = lax.broadcasted_iota(jnp.int32, (nodes, nodes), 1)
    rank = jnp.sum(((dest_row == dest_col) & (sub < lane)).astype(jnp.int32), axis=0, keepdims=True)
    place_row = dest_row * slots + rank
    chosen = (
        lax.broadcasted_iota(jnp.int32, (wide * slots, nodes), 0) == place_row
    ).astype(f32).astype(bf16)
    where_to = (perm_col - dest_col * nodes == lane).astype(f32).astype(bf16)
    pack[:, hidden:] = dot(chosen, where_to, (1, 0)).astype(bf16)

    for copy in inputs[4:8]:
        copy.wait()
    weight_t = weight[...].astype(f32).T.astype(bf16)
    bias_t = jnp.broadcast_to(bias[...], (nodes, hidden)).T
    classes = cls.shape[0]
    cpad[:classes, :] = cls[...]
    cls_t = cpad[...].astype(f32).T.astype(bf16)

    for k in range(Y - 1):
        slot = xl * Y + ring_from(y, k, Y)
        fy(k, slot).wait_recv()
        fx(k, slot).start()
    table_copy.wait()
    inputs[8].wait()
    for k in range(Y):
        fx(k, (1 - xl) * Y + ring_from(y, k, Y)).wait_recv()

    def aggregate(b):
        left = jnp.concatenate([ft[table[0, b]], ft[table[1, b]]], axis=1)
        right = jnp.concatenate([tiles[2 * b], tiles[2 * b + 1]], axis=1)
        return dot(left, right, (1, 1))

    parts = (pl.ds(0, 5), pl.ds(5, Z - 5))

    def s_copy(g, p):
        return rcopy(sbuf.at[g, parts[p]], srecv.at[g, parts[p]], s_s.at[g, p], s_r.at[g, p], s_dev)

    def x_copy(p):
        span = (pl.ds(0, 2), pl.ds(2, 5))[p]
        return rcopy(xbuf.at[span], xrecv.at[span], x_s.at[p], x_r.at[p], x_dev)

    def far_copy(g, k):
        relay = FAR[k] - RELAY if FAR[k] > 0 else FAR[k] + RELAY
        return rcopy(fbuf.at[g, k], frecv.at[g, k], f_s.at[g, k], f_r.at[g, k], z_dev(relay))

    def z_copy(k):
        return rcopy(zbuf.at[k], zrecv.at[k], z_s.at[k], z_r.at[k], z_dev(NEAR[k]))

    columns = (1 - xh, xh)
    spans = (range(5), range(5, Z))

    def for_sibling(g, p):
        for k in spans[p]:
            sbuf[g, k] = aggregate(nid(columns[g], zat(INWARD[k], -1), 1 - c)).astype(bf16)
        s_copy(g, p).start()

    def for_own(g, p):
        for k in spans[p]:
            own[g, k] = aggregate(nid(columns[g], zat(INWARD[k]), c))

    def chip_sum(g, k):
        return own[g, k] + srecv[g, k].astype(f32)

    def add_far(g, k, part):
        for u in range(5):
            if FAR[u] * NEAR[k] > 0:
                far_copy(g, u).wait_recv()
                part = part + frecv[g, u].astype(f32)
        return part

    for p in range(2):
        for g in range(2):
            for_sibling(g, p)
        for g in range(2):
            for_own(g, p)
    for g in range(2):
        s_copy(g, 0).wait_recv()
        for k in range(5):
            fbuf[g, k] = chip_sum(g, k).astype(bf16)
            far_copy(g, k).start()
    s_copy(0, 1).wait_recv()
    s_copy(1, 1).wait_recv()
    for k in range(2, 7):
        xbuf[k] = chip_sum(0, k + 5).astype(bf16)
    x_copy(1).start()
    for k in range(2):
        xbuf[k] = add_far(0, k, chip_sum(0, k + 5)).astype(bf16)
    x_copy(0).start()
    x_copy(1).wait_recv()
    for k in range(2, 6):
        zbuf[k] = (chip_sum(1, k + 5) + xrecv[k].astype(f32)).astype(bf16)
        z_copy(k).start()
    sums = [add_far(1, k, chip_sum(1, k + 5)) for k in range(2)]
    x_copy(0).wait_recv()
    for k in range(2):
        zbuf[k] = (sums[k] + xrecv[k].astype(f32)).astype(bf16)
        z_copy(k).start()
    total = chip_sum(1, Z - 1) + xrecv[6].astype(f32)
    for k in (2, 3, 4, 5, 0, 1):
        z_copy(k).wait_recv()
        total = total + zrecv[k].astype(f32)

    def wait_forward():
        for k in range(Y):
            fx(k, w).wait_send()
            if k < Y - 1:
                fy(k, w).wait_send()
        for p in range(2):
            s_copy(0, p).wait_send()
            s_copy(1, p).wait_send()
            x_copy(p).wait_send()
        for k in range(5):
            far_copy(0, k).wait_send()
            far_copy(1, k).wait_send()
        for k in range(6):
            z_copy(k).wait_send()


    hidden_pre = split_dot(weight_t, total) + bias_t
    gate_value = jax.nn.sigmoid(hidden_pre)
    activated = (hidden_pre * gate_value).astype(bf16)
    class_id = lax.broadcasted_iota(jnp.int32, (cpad.shape[0], nodes), 0)
    logits = dot(cpad[...], activated, (1, 0))
    logits = jnp.where(class_id < classes, logits, -jnp.inf)
    top_score = jnp.max(logits, axis=0, keepdims=True)
    shifted = jnp.exp(logits - top_score)
    exp_total = jnp.sum(shifted, axis=0, keepdims=True)
    target = class_id == labels[...]
    grad_logits = shifted / exp_total - target.astype(f32)
    grad_act = split_dot(cls_t, grad_logits)
    grad_pre = (grad_act * gate_value * (1.0 + hidden_pre * (1.0 - gate_value))).astype(bf16)
    gbuf[n] = dot(weight[...], grad_pre, (1, 0)).astype(bf16)

    def gz(g, offset, slot, towards):
        k = INWARD.index(offset)
        return rcopy(gbuf.at[slot], gbuf.at[slot], gz_s.at[g, k], gz_r.at[g, k], z_dev(towards))

    def gx(offset, slot):
        k = INWARD.index(offset)
        return rcopy(gbuf.at[slot], gbuf.at[slot], gx_s.at[k], gx_r.at[k], x_dev)

    def gs(g, offset, slot):
        k = INWARD.index(offset)
        return rcopy(gbuf.at[slot], gbuf.at[slot], gs_s.at[g, k], gs_r.at[g, k], s_dev)

    def pass_on(g, offset, slot):
        if offset == -RELAY:
            for further, seen_at in ((3, 6), (2, -5), (1, -4)):
                gz(g, seen_at, slot, further).start()
        if offset == RELAY:
            for further, seen_at in ((-2, 5), (-1, 4)):
                gz(g, seen_at, slot, further).start()

    gx(0, n).start()
    for offset in (3, -3, 1, -1, 2, -2):
        gz(0, -offset, n, offset).start()
    gs(0, 0, n).start()

    pack[:, :hidden] = dot(chosen, activated, (1, 1)).astype(bf16)

    def a_copy(d, src, dst):
        return rcopy(
            pack.at[pl.ds(src * slots, slots)], unpack.at[pl.ds(dst * slots, slots)],
            a_s.at[d], a_r.at[d], w_dev(d),
        )

    for d in range(1, wide):
        a_copy(d, ring_step(w, d, wide), w).start()
    mine = pl.ds(pl.multiple_of(w * slots, slots), slots)
    unpack[mine, :] = pack[mine, :]
    picked = jnp.sum(jnp.where(target, logits, 0.0), axis=0, keepdims=True)
    loss_ref[...] = top_score + jnp.log(exp_total) - picked

    wait_forward()

    def spread(b):
        right = jnp.concatenate([tiles[2 * b], tiles[2 * b + 1]], axis=1)
        part = dot(gbuf[b], right, (1, 0))
        for t in range(2):
            run[2 * b + t + 1] = part[:, t * nodes : (t + 1) * nodes] + run[table[2 + t, b]]

    ready = []
    for i in range(len(ARRIVALS) + SIBLING_LAG):
        if i < len(ARRIVALS):
            kind, offset = ARRIVALS[i]
            g = int(kind != "own")
            slot = nid(xh if g == 0 else 1 - xh, zat(offset), c)
            if kind == "x":
                gx(offset, slot).wait_recv()
                pass_on(1, offset, slot)
                gs(1, offset, slot).start()
            elif offset:
                gz(g, offset, slot, 1).wait_recv()
                if kind == "own":
                    pass_on(0, offset, slot)
                    if offset in NEAR:
                        gx(offset, slot).start()
                gs(g, offset, slot).start()
            ready.append(slot)
        if i >= SIBLING_LAG:
            kind, offset = ARRIVALS[i - SIBLING_LAG]
            g = int(kind != "own")
            slot = nid(xh if g == 0 else 1 - xh, zat(offset, -1), 1 - c)
            gs(g, offset, slot).wait_recv()
            ready.append(slot)
        if i % 4 == 3 or i == len(ARRIVALS) + SIBLING_LAG - 1:
            for slot in ready:
                spread(slot)
            ready = []

    def wait_backward():
        for d in range(1, wide):
            a_copy(d, ring_step(w, d, wide), w).wait_send()
        for offset in INWARD:
            gs(0, offset, n).wait_send()
            gs(1, offset, n).wait_send()
            if offset in NEAR:
                gx(offset, n).wait_send()
            else:
                gz(1, offset, n, 1).wait_send()
            if offset:
                gz(0, offset, n, 1).wait_send()

    def place():
        for d in range(1, wide):
            a_copy(d, w, ring_step(w, -d, wide)).wait_recv()
        next_ref[...] = dot(unpack[:, hidden:], unpack[:, :hidden], (0, 0)).astype(bf16)


    def cx(k):
        return rcopy(cxbuf.at[k], cxrecv.at[k], cx_s.at[k], cx_r.at[k], xl_dev)

    def cy(k):
        return rcopy(cybuf.at[k], cyrecv.at[k], cy_s.at[k], cy_r.at[k], (xl * Y + ring_step(y, Y_FAR[k], Y), n))

    def cn(g, k):
        return rcopy(
            cnbuf.at[g, k], cnrecv.at[g, k], cn_s.at[g, k], cn_r.at[g, k], (xl * Y + ring_step(y, Y_NEAR[k], Y), n)
        )

    def column_sum(g, offset):
        return run[table[4, (xl if g else 1 - xl) * Y + ring_step(y, offset, Y)]]

    for k in range(3):
        cxbuf[k] = column_sum(0, Y_FAR[k]).astype(bf16)
        cx(k).start()
    for g in range(2):
        for k in range(4):
            cnbuf[g, k] = column_sum(g, Y_NEAR[k]).astype(bf16)
            cn(g, k).start()
    for k in range(3):
        part = column_sum(1, Y_FAR[k])
        cx(k).wait_recv()
        cybuf[k] = (part + cxrecv[k].astype(f32)).astype(bf16)
        cy(k).start()
    part = column_sum(0, 0)
    for k in range(4):
        cn(0, k).wait_recv()
        part = part + cnrecv[0, k].astype(f32)
    cxbuf[3] = part.astype(bf16)
    cx(3).start()

    place()
    wait_backward()

    part = column_sum(1, 0)
    for k in range(4):
        cn(1, k).wait_recv()
        part = part + cnrecv[1, k].astype(f32)
    for k in range(3):
        cy(k).wait_recv()
        part = part + cyrecv[k].astype(f32)
    cx(3).wait_recv()
    part = part + cxrecv[3].astype(f32)
    grad_ref[...] = part.T

    for k in range(4):
        cx(k).wait_send()
        cn(0, k).wait_send()
        cn(1, k).wait_send()
        if k < 3:
            cy(k).wait_send()


def deliver_kernel(*refs):
    sems = refs[-1]
    copies = [pltpu.make_async_copy(refs[i], refs[i + 3], sems.at[i]) for i in range(3)]
    for copy in copies:
        copy.start()
    for copy in copies:
        copy.wait()


def per_device(
    wide, narrow, features, in_weight, hidden_bias, classifier, adjacency_tiles, tile_col, tile_count, node_perm, labels
):
    nodes, f_in = features.shape[1], features.shape[2]
    hidden = in_weight.shape[1]
    tile = adjacency_tiles.shape[3]
    Y, Z = wide // 2, narrow // 4
    padded = -(-classifier.shape[1] // 128) * 128
    slots = 16
    block = (f_in, tile)
    vmem = pl.BlockSpec(memory_space=pltpu.VMEM)
    hbm = pl.BlockSpec(memory_space=pltpu.HBM)
    dma = pltpu.SemaphoreType.DMA
    results = pl.pallas_call(
        functools.partial(layer_kernel, wide, narrow),
        out_shape=(
            pltpu.VMEM((nodes, hidden), bf16),
            pltpu.VMEM((1, nodes), f32),
            pltpu.VMEM((nodes, f_in), f32),
        ),
        in_specs=[hbm] * 9,
        out_specs=(vmem, vmem, vmem),
        scratch_shapes=[
            pltpu.VMEM((nodes, f_in), bf16),
            pltpu.VMEM((f_in, hidden), bf16),
            pltpu.VMEM((1, hidden), f32),
            pltpu.VMEM(classifier.shape[::-1], bf16),
            pltpu.VMEM((narrow * 2, tile, tile), bf16),
            pltpu.VMEM((2, narrow), jnp.int32),
            pltpu.VMEM((1, narrow), jnp.int32),
            pltpu.VMEM((1, nodes), jnp.int32),
            pltpu.VMEM((1, nodes), jnp.int32),
            pltpu.VMEM((8, nodes), jnp.int32),
            pltpu.SMEM((8, nodes), jnp.int32),
            pltpu.VMEM((wide + 1,) + block, bf16),
            pltpu.VMEM((2, Z) + block, bf16),
            pltpu.VMEM((2, Z) + block, bf16),
            pltpu.VMEM((2, 5) + block, bf16),
            pltpu.VMEM((2, 5) + block, bf16),
            pltpu.VMEM((7,) + block, bf16),
            pltpu.VMEM((7,) + block, bf16),
            pltpu.VMEM((6,) + block, bf16),
            pltpu.VMEM((6,) + block, bf16),
            pltpu.VMEM((2, Z) + block, f32),
            pltpu.VMEM((narrow,) + block, bf16),
            pltpu.VMEM((narrow * 2 + 1,) + block, f32),
            pltpu.VMEM((wide * slots, hidden + nodes), bf16),
            pltpu.VMEM((wide * slots, hidden + nodes), bf16),
            pltpu.VMEM((4,) + block, bf16),
            pltpu.VMEM((4,) + block, bf16),
            pltpu.VMEM((3,) + block, bf16),
            pltpu.VMEM((3,) + block, bf16),
            pltpu.VMEM((2, 4) + block, bf16),
            pltpu.VMEM((2, 4) + block, bf16),
            pltpu.VMEM((padded, hidden), bf16),
            dma((9,)), dma,
            dma((Y - 1,)), dma((Y - 1,)), dma((Y,)), dma((Y,)),
            dma((2, 2)), dma((2, 2)), dma((2, 5)), dma((2, 5)), dma((2,)), dma((2,)), dma((6,)), dma((6,)),
            dma((2, Z)), dma((2, Z)), dma((Z,)), dma((Z,)), dma((2, Z)), dma((2, Z)),
            dma((4,)), dma((4,)), dma((3,)), dma((3,)), dma((2, 4)), dma((2, 4)), dma((wide,)), dma((wide,)),
        ],
        compiler_params=pltpu.CompilerParams(
            collective_id=0, has_side_effects=True, vmem_limit_bytes=61 * 2**20
        ),
        name="layer",
    )(
        features.reshape(nodes, f_in), in_weight, hidden_bias.reshape(1, hidden), classifier.T,
        adjacency_tiles.reshape(-1, tile, tile), tile_col.transpose(1, 2, 0).reshape(-1, narrow),
        tile_count.reshape(1, narrow), node_perm, labels.reshape(1, nodes),
    )
    next_rows, node_loss, input_grad = pl.pallas_call(
        deliver_kernel,
        out_shape=[jax.ShapeDtypeStruct(result.shape, result.dtype) for result in results],
        in_specs=[vmem] * 3,
        out_specs=[hbm] * 3,
        scratch_shapes=[dma((3,))],
        compiler_params=pltpu.CompilerParams(vmem_limit_bytes=2**20),
        name="deliver",
    )(*results)
    return next_rows.reshape(1, nodes, hidden), node_loss.reshape(nodes), input_grad.reshape(1, nodes, f_in)


def solution(mesh):
    in_specs = (
        P("narrow", "wide", None),
        P(),
        P(),
        P(),
        P("wide", "narrow", None, None, None),
        P("wide", "narrow", None),
        P("wide", "narrow"),
        P("narrow", "wide"),
        P(("wide", "narrow")),
    )
    out_specs = (P("narrow", "wide", None), P(("wide", "narrow")), P("narrow", "wide", None))
    return jax.shard_map(
        functools.partial(per_device, mesh.shape["wide"], mesh.shape["narrow"]),
        mesh=mesh, in_specs=in_specs, out_specs=out_specs, check_vma=False,
    )
```

```python
import functools

import jax
import jax.numpy as jnp
from jax import lax
from jax.experimental import pallas as pl
from jax.experimental.pallas import tpu as pltpu
from jax.sharding import PartitionSpec as P

MESH = pl.DeviceIdType.MESH
RELAY = 3
INWARD = (6, 5, -5, 4, -4, 3, -3, 2, -2, 1, -1, 0)
FAR, NEAR = INWARD[:5], INWARD[5:]
Y_FAR, Y_NEAR = (4, 3, -3), (2, -2, 1, -1)
ARRIVALS = (
    ("own", 0), ("own", 3), ("own", -3), ("own", 1), ("own", -1), ("x", 0), ("own", 2), ("own", -2),
    ("x", 3), ("x", -3), ("x", 1), ("x", -1), ("own", 4), ("own", -4), ("own", 5), ("own", -5), ("own", 6),
    ("x", 2), ("x", -2), ("other", 4), ("other", -4), ("other", 5), ("other", -5), ("other", 6),
)
GROUPS = (
    (0, 1), (1, 3), (3, 5), (5, 6), (6, 8), (8, 10), (10, 12), (12, 14), (14, 17), (17, 19), (19, 21), (21, 23), (23, 24),
)
SIBLING_LAG = 6


def due(i):
    return [p for p, (first, end) in enumerate(GROUPS) if end - 1 == i - SIBLING_LAG]


def spread_order():
    order = []
    for i in range(len(ARRIVALS) + SIBLING_LAG):
        steps = [(i, 0)] if i < len(ARRIVALS) else []
        steps += [(j, 1) for p in due(i) for j in range(*GROUPS[p])]
        for j, sibling in steps:
            kind, offset = ARRIVALS[j]
            order.append((int(kind != "own"), sibling, offset))
    return order


f32, bf16 = jnp.float32, jnp.bfloat16


def ring_offset(k, size):
    steps = size // 2 - (k + 1) // 2
    return steps * ((k % 2) * 2 - 1)


def ring_step(place, offset, size):
    moved = place + offset
    if offset > 0:
        return jnp.where(moved >= size, moved - size, moved)
    return jnp.where(moved < 0, moved + size, moved) if offset else place


def ring_to(place, k, size):
    return ring_step(place, ring_offset(k, size), size)


def ring_from(place, k, size):
    return ring_step(place, -ring_offset(k, size), size)


def dot(a, b, contract):
    return lax.dot_general(a, b, ((contract[:1], contract[1:]), ((), ())), preferred_element_type=f32)


def split_dot(a, b):
    high = b.astype(bf16)
    low = (b - high.astype(f32)).astype(bf16)
    return dot(a, high, (1, 0)) + dot(a, low, (1, 0))


def turned(row, size):
    return jnp.broadcast_to(row.astype(f32), (size, size)).T.astype(jnp.int32)


def layer_kernel(
    wide, narrow,
    feat_hbm, weight_hbm, bias_hbm, cls_hbm, tiles_hbm, cols_hbm, counts_hbm, perm_hbm, labels_hbm,
    next_ref, loss_ref, grad_ref,
    feat, weight, bias, cls, tiles, cols, counts, perm, labels, table_v, table,
    ft, sbuf, srecv, fbuf, frecv, xbuf, xrecv, zbuf, zrecv, own, gbuf, gsib, run,
    pack, unpack, cxbuf, cxrecv, cybuf, cyrecv, cnbuf, cnrecv, cpad,
    in_sem, table_sem, fy_s, fy_r, fx_s, fx_r, s_s, s_r, f_s, f_r, x_s, x_r, z_s, z_r,
    g_s, g_r, gs_s, gs_r, cx_s, cx_r, cy_s, cy_r, cn_s, cn_r, a_s, a_r,
):
    Y, Z = wide // 2, narrow // 4
    w, n = lax.axis_index("wide"), lax.axis_index("narrow")
    xl, y = w // Y, w % Y
    xh, z, c = n // (2 * Z), (n // 2) % Z, n % 2

    def nid(xh_, z_, c_):
        return (xh_ * Z + z_) * 2 + c_

    def rcopy(src, dst, ss, rs, dev):
        return pltpu.make_async_remote_copy(
            src_ref=src, dst_ref=dst, send_sem=ss, recv_sem=rs, device_id=dev, device_id_type=MESH
        )

    x_dev = (w, nid(1 - xh, z, c))
    s_dev = (w, nid(xh, z, 1 - c))
    xl_dev = ((1 - xl) * Y + y, n)

    sign = 1 - 2 * c

    def zat(offset, facing=1):
        moved = z + sign * (facing * offset)
        return jnp.where(moved < 0, moved + Z, jnp.where(moved >= Z, moved - Z, moved))

    def z_dev(offset):
        return (w, nid(xh, zat(offset), c))

    def y_dev(k):
        return (xl * Y + ring_to(y, k, Y), n)

    def w_dev(d):
        return (ring_step(w, d, wide), n)

    barrier = pltpu.get_barrier_semaphore()
    partners = [w_dev(d) for d in range(1, wide)] + [z_dev(o) for o in (1, -1, 2, -2, 3, -3)] + [x_dev, s_dev]
    for partner in partners:
        pl.semaphore_signal(barrier, inc=1, device_id=partner, device_id_type=MESH)

    inputs = [
        pltpu.make_async_copy(src, dst, in_sem.at[i])
        for i, (src, dst) in enumerate((
            (feat_hbm, feat), (cols_hbm, cols), (counts_hbm, counts), (perm_hbm, perm), (weight_hbm, weight),
            (bias_hbm, bias), (cls_hbm, cls), (labels_hbm, labels), (tiles_hbm, tiles),
        ))
    ]
    for copy in inputs:
        copy.start()
    run[0] = jnp.zeros_like(run[0])
    ft[wide] = jnp.zeros_like(ft[wide])
    table_v[...] = jnp.full(table_v.shape, -1, jnp.int32)
    cpad[...] = jnp.zeros_like(cpad)
    inputs[0].wait()
    ft[w] = feat[...].astype(f32).T.astype(bf16)

    for copy in inputs[1:4]:
        copy.wait()
    nodes = perm.shape[1]
    table_v[0:2, :narrow] = cols[...]
    table_v[2:3, :narrow] = counts[...]
    lane_row = lax.broadcasted_iota(jnp.int32, (1, nodes), 1)
    in_upper = (lane_row >= 2 * Z).astype(jnp.int32)
    in_half = lane_row - 2 * Z * in_upper
    far = ((in_half >> 1) - z) * (1 - 2 * (in_half & 1))
    far = jnp.where(far < 0, far + Z, far)
    other_x, other_c = jnp.abs(in_upper - xh), jnp.abs((in_half & 1) - c)
    kind = (other_x * 2 + other_c) * Z + far
    when = jnp.zeros_like(far)
    for turn, (column_, core, offset) in enumerate(spread_order()):
        when = jnp.where(kind == (column_ * 2 + core) * Z + offset % Z, turn, when)
    column = [table_v[0:1, :], jnp.where(table_v[2:3, :] > 1, table_v[1:2, :], jnp.where(lane_row < narrow, wide, -1))]
    key = [when * 256 + 2 * lane_row + 1 + t for t in range(2)]
    column_down = [turned(row, nodes) for row in column]
    key_down = [turned(row, nodes) for row in key]
    for t in range(2):
        fits = [
            jnp.where((column_down[u] == column[t]) & (key_down[u] < when * 256), key_down[u], 0) for u in range(2)
        ]
        table_v[2 + t : 3 + t, :] = jnp.max(jnp.maximum(fits[0], fits[1]), axis=0, keepdims=True) & 255
    fits = [jnp.where(column_down[u] == lane_row, key_down[u], 0) for u in range(2)]
    table_v[4:5, :] = jnp.max(jnp.maximum(fits[0], fits[1]), axis=0, keepdims=True) & 255
    table_v[1:2, :] = column[1]
    table_copy = pltpu.make_async_copy(table_v, table, table_sem)
    table_copy.start()

    pl.semaphore_wait(barrier, len(partners))

    def fy(k, slot):
        return rcopy(ft.at[slot], ft.at[slot], fy_s.at[k], fy_r.at[k], y_dev(k))

    def fx(k, slot):
        return rcopy(ft.at[slot], ft.at[slot], fx_s.at[k], fx_r.at[k], xl_dev)

    fx(Y - 1, w).start()
    for k in range(Y - 1):
        fy(k, w).start()

    slots = unpack.shape[0] // wide
    hidden = bias.shape[1]
    perm_row = perm[...]
    shift = nodes.bit_length() - 1
    dest_row, perm_col = perm_row >> shift, turned(perm_row, nodes)
    dest_col = perm_col >> shift
    sub = lax.broadcasted_iota(jnp.int32, (nodes, nodes), 0)
    lane = lax.broadcasted_iota(jnp.int32, (nodes, nodes), 1)
    rank = jnp.sum(((dest_row == dest_col) & (sub < lane)).astype(jnp.int32), axis=0, keepdims=True)
    place_row = dest_row * slots + rank
    chosen = (
        lax.broadcasted_iota(jnp.int32, (wide * slots, nodes), 0) == place_row
    ).astype(f32).astype(bf16)
    where_to = (perm_col - dest_col * nodes == lane).astype(f32).astype(bf16)
    pack[:, hidden:] = dot(chosen, where_to, (1, 0)).astype(bf16)

    for copy in inputs[4:8]:
        copy.wait()
    weight_t = weight[...].astype(f32).T.astype(bf16)
    bias_t = jnp.broadcast_to(bias[...], (nodes, hidden)).T
    classes = cls.shape[0]
    cpad[:classes, :] = cls[...]
    cls_t = cpad[...].astype(f32).T.astype(bf16)

    for k in range(Y - 1):
        slot = xl * Y + ring_from(y, k, Y)
        fy(k, slot).wait_recv()
        fx(k, slot).start()
    table_copy.wait()
    inputs[8].wait()
    for k in range(Y):
        fx(k, (1 - xl) * Y + ring_from(y, k, Y)).wait_recv()

    def aggregate(b):
        left = jnp.concatenate([ft[table[0, b]], ft[table[1, b]]], axis=1)
        right = jnp.concatenate([tiles[2 * b], tiles[2 * b + 1]], axis=1)
        return dot(left, right, (1, 1))

    parts = (pl.ds(0, 5), pl.ds(5, Z - 5))

    def s_copy(g, p):
        return rcopy(sbuf.at[g, parts[p]], srecv.at[g, parts[p]], s_s.at[g, p], s_r.at[g, p], s_dev)

    def x_copy(p):
        span = (pl.ds(0, 2), pl.ds(2, 5))[p]
        return rcopy(xbuf.at[span], xrecv.at[span], x_s.at[p], x_r.at[p], x_dev)

    def far_copy(g, k):
        relay = FAR[k] - RELAY if FAR[k] > 0 else FAR[k] + RELAY
        return rcopy(fbuf.at[g, k], frecv.at[g, k], f_s.at[g, k], f_r.at[g, k], z_dev(relay))

    def z_copy(k):
        return rcopy(zbuf.at[k], zrecv.at[k], z_s.at[k], z_r.at[k], z_dev(NEAR[k]))

    columns = (1 - xh, xh)
    spans = (range(5), range(5, Z))

    def for_sibling(g, p):
        for k in spans[p]:
            sbuf[g, k] = aggregate(nid(columns[g], zat(INWARD[k], -1), 1 - c)).astype(bf16)
        s_copy(g, p).start()

    def for_own(g, p):
        for k in spans[p]:
            own[g, k] = aggregate(nid(columns[g], zat(INWARD[k]), c))

    def chip_sum(g, k):
        return own[g, k] + srecv[g, k].astype(f32)

    def add_far(g, k, part):
        for u in range(5):
            if FAR[u] * NEAR[k] > 0:
                far_copy(g, u).wait_recv()
                part = part + frecv[g, u].astype(f32)
        return part

    for p in range(2):
        for g in range(2):
            for_sibling(g, p)
        for g in range(2):
            for_own(g, p)
    for g in range(2):
        s_copy(g, 0).wait_recv()
        for k in range(5):
            fbuf[g, k] = chip_sum(g, k).astype(bf16)
            far_copy(g, k).start()
    s_copy(0, 1).wait_recv()
    s_copy(1, 1).wait_recv()
    for k in range(2, 7):
        xbuf[k] = chip_sum(0, k + 5).astype(bf16)
    x_copy(1).start()
    for k in range(2):
        xbuf[k] = add_far(0, k, chip_sum(0, k + 5)).astype(bf16)
    x_copy(0).start()
    x_copy(1).wait_recv()
    for k in range(2, 6):
        zbuf[k] = (chip_sum(1, k + 5) + xrecv[k].astype(f32)).astype(bf16)
        z_copy(k).start()
    sums = [add_far(1, k, chip_sum(1, k + 5)) for k in range(2)]
    x_copy(0).wait_recv()
    for k in range(2):
        zbuf[k] = (sums[k] + xrecv[k].astype(f32)).astype(bf16)
        z_copy(k).start()
    total = chip_sum(1, Z - 1) + xrecv[6].astype(f32)
    for k in (2, 3, 4, 5, 0, 1):
        z_copy(k).wait_recv()
        total = total + zrecv[k].astype(f32)

    def wait_forward():
        for k in range(Y):
            fx(k, w).wait_send()
            if k < Y - 1:
                fy(k, w).wait_send()
        for p in range(2):
            s_copy(0, p).wait_send()
            s_copy(1, p).wait_send()
            x_copy(p).wait_send()
        for k in range(5):
            far_copy(0, k).wait_send()
            far_copy(1, k).wait_send()
        for k in range(6):
            z_copy(k).wait_send()


    hidden_pre = split_dot(weight_t, total) + bias_t
    gate_value = jax.nn.sigmoid(hidden_pre)
    activated = (hidden_pre * gate_value).astype(bf16)
    class_id = lax.broadcasted_iota(jnp.int32, (cpad.shape[0], nodes), 0)
    logits = dot(cpad[...], activated, (1, 0))
    logits = jnp.where(class_id < classes, logits, -jnp.inf)
    top_score = jnp.max(logits, axis=0, keepdims=True)
    shifted = jnp.exp(logits - top_score)
    exp_total = jnp.sum(shifted, axis=0, keepdims=True)
    target = class_id == labels[...]
    grad_logits = shifted / exp_total - target.astype(f32)
    grad_act = split_dot(cls_t, grad_logits)
    grad_pre = (grad_act * gate_value * (1.0 + hidden_pre * (1.0 - gate_value))).astype(bf16)
    gbuf[0] = dot(weight[...], grad_pre, (1, 0)).astype(bf16)

    def hand(source, kind, offset, towards):
        j = ARRIVALS.index((kind, offset))
        device = x_dev if kind == "x" else z_dev(towards)
        return rcopy(gbuf.at[source], gbuf.at[j], g_s.at[j], g_r.at[j], device)

    def gs(p):
        span = pl.ds(GROUPS[p][0], GROUPS[p][1] - GROUPS[p][0])
        return rcopy(gbuf.at[span], gsib.at[span], gs_s.at[p], gs_r.at[p], s_dev)

    def pass_on(j):
        kind, offset = ARRIVALS[j]
        into = "own" if kind == "own" else "other"
        if offset == -RELAY:
            for further, seen_at in ((3, 6), (2, -5), (1, -4)):
                hand(j, into, seen_at, further).start()
        if offset == RELAY:
            for further, seen_at in ((-2, 5), (-1, 4)):
                hand(j, into, seen_at, further).start()

    hand(0, "x", 0, 0).start()
    for offset in (3, -3, 1, -1, 2, -2):
        hand(0, "own", -offset, offset).start()
    gs(0).start()

    pack[:, :hidden] = dot(chosen, activated, (1, 1)).astype(bf16)

    def a_copy(d, src, dst):
        return rcopy(
            pack.at[pl.ds(src * slots, slots)], unpack.at[pl.ds(dst * slots, slots)],
            a_s.at[d], a_r.at[d], w_dev(d),
        )

    for d in range(1, wide):
        a_copy(d, ring_step(w, d, wide), w).start()
    mine = pl.ds(pl.multiple_of(w * slots, slots), slots)
    unpack[mine, :] = pack[mine, :]
    picked = jnp.sum(jnp.where(target, logits, 0.0), axis=0, keepdims=True)
    loss_ref[...] = top_score + jnp.log(exp_total) - picked

    wait_forward()

    def spread(j, sibling):
        kind, offset = ARRIVALS[j]
        column_ = xh if kind == "own" else 1 - xh
        b = nid(column_, zat(offset, -1), 1 - c) if sibling else nid(column_, zat(offset), c)
        right = jnp.concatenate([tiles[2 * b], tiles[2 * b + 1]], axis=1)
        part = dot(gsib[j] if sibling else gbuf[j], right, (1, 0))
        for t in range(2):
            run[2 * b + t + 1] = part[:, t * nodes : (t + 1) * nodes] + run[table[2 + t, b]]

    ready = []
    for i in range(len(ARRIVALS) + SIBLING_LAG):
        if i < len(ARRIVALS):
            kind, offset = ARRIVALS[i]
            if i:
                hand(i, kind, offset, 1).wait_recv()
                if kind != "other":
                    pass_on(i)
                if kind == "own" and offset in NEAR:
                    hand(i, "x", offset, 0).start()
                for p, (first, end) in enumerate(GROUPS):
                    if end - 1 == i:
                        gs(p).start()
            ready.append((i, False))
        for p in due(i):
            gs(p).wait_recv()
            ready += [(j, True) for j in range(*GROUPS[p])]
        if i % 4 == 3 or i == len(ARRIVALS) + SIBLING_LAG - 1:
            for j, sibling in ready:
                spread(j, sibling)
            ready = []

    def wait_backward():
        for d in range(1, wide):
            a_copy(d, ring_step(w, d, wide), w).wait_send()
        for j in range(1, len(ARRIVALS)):
            hand(0, *ARRIVALS[j], 1).wait_send()
        for p in range(len(GROUPS)):
            gs(p).wait_send()

    def place():
        for d in range(1, wide):
            a_copy(d, w, ring_step(w, -d, wide)).wait_recv()
        next_ref[...] = dot(unpack[:, hidden:], unpack[:, :hidden], (0, 0)).astype(bf16)


    def cx(k):
        return rcopy(cxbuf.at[k], cxrecv.at[k], cx_s.at[k], cx_r.at[k], xl_dev)

    def cy(k):
        return rcopy(cybuf.at[k], cyrecv.at[k], cy_s.at[k], cy_r.at[k], (xl * Y + ring_step(y, Y_FAR[k], Y), n))

    def cn(g, k):
        return rcopy(
            cnbuf.at[g, k], cnrecv.at[g, k], cn_s.at[g, k], cn_r.at[g, k], (xl * Y + ring_step(y, Y_NEAR[k], Y), n)
        )

    def column_sum(g, offset):
        return run[table[4, (xl if g else 1 - xl) * Y + ring_step(y, offset, Y)]]

    for k in range(3):
        cxbuf[k] = column_sum(0, Y_FAR[k]).astype(bf16)
        cx(k).start()
    for g in range(2):
        for k in range(4):
            cnbuf[g, k] = column_sum(g, Y_NEAR[k]).astype(bf16)
            cn(g, k).start()
    for k in range(3):
        part = column_sum(1, Y_FAR[k])
        cx(k).wait_recv()
        cybuf[k] = (part + cxrecv[k].astype(f32)).astype(bf16)
        cy(k).start()
    part = column_sum(0, 0)
    for k in range(4):
        cn(0, k).wait_recv()
        part = part + cnrecv[0, k].astype(f32)
    cxbuf[3] = part.astype(bf16)
    cx(3).start()

    place()
    wait_backward()

    part = column_sum(1, 0)
    for k in range(4):
        cn(1, k).wait_recv()
        part = part + cnrecv[1, k].astype(f32)
    for k in range(3):
        cy(k).wait_recv()
        part = part + cyrecv[k].astype(f32)
    cx(3).wait_recv()
    part = part + cxrecv[3].astype(f32)
    grad_ref[...] = part.T

    for k in range(4):
        cx(k).wait_send()
        cn(0, k).wait_send()
        cn(1, k).wait_send()
        if k < 3:
            cy(k).wait_send()


def deliver_kernel(*refs):
    sems = refs[-1]
    copies = [pltpu.make_async_copy(refs[i], refs[i + 3], sems.at[i]) for i in range(3)]
    for copy in copies:
        copy.start()
    for copy in copies:
        copy.wait()


def per_device(
    wide, narrow, features, in_weight, hidden_bias, classifier, adjacency_tiles, tile_col, tile_count, node_perm, labels
):
    nodes, f_in = features.shape[1], features.shape[2]
    hidden = in_weight.shape[1]
    tile = adjacency_tiles.shape[3]
    Y, Z = wide // 2, narrow // 4
    padded = -(-classifier.shape[1] // 128) * 128
    slots = 16
    block = (f_in, tile)
    vmem = pl.BlockSpec(memory_space=pltpu.VMEM)
    hbm = pl.BlockSpec(memory_space=pltpu.HBM)
    dma = pltpu.SemaphoreType.DMA
    results = pl.pallas_call(
        functools.partial(layer_kernel, wide, narrow),
        out_shape=(
            pltpu.VMEM((nodes, hidden), bf16),
            pltpu.VMEM((1, nodes), f32),
            pltpu.VMEM((nodes, f_in), f32),
        ),
        in_specs=[hbm] * 9,
        out_specs=(vmem, vmem, vmem),
        scratch_shapes=[
            pltpu.VMEM((nodes, f_in), bf16),
            pltpu.VMEM((f_in, hidden), bf16),
            pltpu.VMEM((1, hidden), f32),
            pltpu.VMEM(classifier.shape[::-1], bf16),
            pltpu.VMEM((narrow * 2, tile, tile), bf16),
            pltpu.VMEM((2, narrow), jnp.int32),
            pltpu.VMEM((1, narrow), jnp.int32),
            pltpu.VMEM((1, nodes), jnp.int32),
            pltpu.VMEM((1, nodes), jnp.int32),
            pltpu.VMEM((8, nodes), jnp.int32),
            pltpu.SMEM((8, nodes), jnp.int32),
            pltpu.VMEM((wide + 1,) + block, bf16),
            pltpu.VMEM((2, Z) + block, bf16),
            pltpu.VMEM((2, Z) + block, bf16),
            pltpu.VMEM((2, 5) + block, bf16),
            pltpu.VMEM((2, 5) + block, bf16),
            pltpu.VMEM((7,) + block, bf16),
            pltpu.VMEM((7,) + block, bf16),
            pltpu.VMEM((6,) + block, bf16),
            pltpu.VMEM((6,) + block, bf16),
            pltpu.VMEM((2, Z) + block, f32),
            pltpu.VMEM((len(ARRIVALS),) + block, bf16),
            pltpu.VMEM((len(ARRIVALS),) + block, bf16),
            pltpu.VMEM((narrow * 2 + 1,) + block, f32),
            pltpu.VMEM((wide * slots, hidden + nodes), bf16),
            pltpu.VMEM((wide * slots, hidden + nodes), bf16),
            pltpu.VMEM((4,) + block, bf16),
            pltpu.VMEM((4,) + block, bf16),
            pltpu.VMEM((3,) + block, bf16),
            pltpu.VMEM((3,) + block, bf16),
            pltpu.VMEM((2, 4) + block, bf16),
            pltpu.VMEM((2, 4) + block, bf16),
            pltpu.VMEM((padded, hidden), bf16),
            dma((9,)), dma,
            dma((Y - 1,)), dma((Y - 1,)), dma((Y,)), dma((Y,)),
            dma((2, 2)), dma((2, 2)), dma((2, 5)), dma((2, 5)), dma((2,)), dma((2,)), dma((6,)), dma((6,)),
            dma((len(ARRIVALS),)), dma((len(ARRIVALS),)), dma((len(GROUPS),)), dma((len(GROUPS),)),
            dma((4,)), dma((4,)), dma((3,)), dma((3,)), dma((2, 4)), dma((2, 4)), dma((wide,)), dma((wide,)),
        ],
        compiler_params=pltpu.CompilerParams(
            collective_id=0, has_side_effects=True, vmem_limit_bytes=61 * 2**20
        ),
        name="layer",
    )(
        features.reshape(nodes, f_in), in_weight, hidden_bias.reshape(1, hidden), classifier.T,
        adjacency_tiles.reshape(-1, tile, tile), tile_col.transpose(1, 2, 0).reshape(-1, narrow),
        tile_count.reshape(1, narrow), node_perm, labels.reshape(1, nodes),
    )
    next_rows, node_loss, input_grad = pl.pallas_call(
        deliver_kernel,
        out_shape=[jax.ShapeDtypeStruct(result.shape, result.dtype) for result in results],
        in_specs=[vmem] * 3,
        out_specs=[hbm] * 3,
        scratch_shapes=[dma((3,))],
        compiler_params=pltpu.CompilerParams(vmem_limit_bytes=2**20),
        name="deliver",
    )(*results)
    return next_rows.reshape(1, nodes, hidden), node_loss.reshape(nodes), input_grad.reshape(1, nodes, f_in)


def solution(mesh):
    in_specs = (
        P("narrow", "wide", None),
        P(),
        P(),
        P(),
        P("wide", "narrow", None, None, None),
        P("wide", "narrow", None),
        P("wide", "narrow"),
        P("narrow", "wide"),
        P(("wide", "narrow")),
    )
    out_specs = (P("narrow", "wide", None), P(("wide", "narrow")), P("narrow", "wide", None))
    return jax.shard_map(
        functools.partial(per_device, mesh.shape["wide"], mesh.shape["narrow"]),
        mesh=mesh, in_specs=in_specs, out_specs=out_specs, check_vma=False,
    )
```
